32 devices in a mesh: outer: 8 (over y, x, core), inner: 4 (over z).
Axes of the slice: x: 2, y: 2, z: 4, core: 2. Of those that a mesh axis runs over, the one named last changes fastest.
Arguments:
- inputs: bfloat16 [4096, 8192], P(('outer', 'inner')), may hold values from -6 to 6
- segment_ids: int32 [32, 128], P(('outer', 'inner')), may hold values from 0 to 7, never falling along the last dimension, each value on 1 to 32 neighbouring positions
- qkv_weight: bfloat16 [8192, 768], P('inner'), may hold values from -0.0625 to 0.0625
- attn_cotangent: bfloat16 [4096, 512], P(('outer', 'inner')), may hold values from -6 to 6
Outputs:
- input_grad: bfloat16 [4096, 8192], P(('outer', 'inner'))
- weight_grad: float32 [8192, 768], P('inner', 'outer')
The draws below stay inside these ranges and needn't reach their ends.
Inputs may be any that keep to these rules, and one draw needn't show every extreme that they name: `segment_ids`: within each sequence the ids never fall, and each id covers one run of 1 to 32 tokens.
All inputs are finite; a program needn't handle non-finite values.
Results may differ from the reference program's by a relative error of at most 0.033.
Values may be sent and summed in bfloat16 or wider, within the bound.
A program may use at most 64 MiB of HBM per device.

```python
import math
import jax
import jax.numpy as jnp
import numpy as np
from jax import lax

D = 8192
HD = 128
QH = 4
SEQ = 128
COLS = 768
SEQS = 32
TOKENS = 4096
N_OUTER = 8
N_INNER = 4


def level_of(own_key, shape, pieces, low, top_value):
    gain = 1.0
    for position, parts in pieces:
        steps = jax.random.uniform(jax.random.fold_in(jax.random.fold_in(own_key, 6), position), (parts,), jnp.float32, low / len(pieces), top_value / len(pieces))
        gain = gain * jnp.repeat(jnp.exp(steps), shape[position] // parts).reshape((-1,) + (1,) * (len(shape) - 1 - position))
    return gain


def split_up(count, total, reach, lean):
    portions = [(1 << 20) // math.isqrt(standing ** lean) + 1 for standing in range(2, count + 1)]
    surplus, given = total - reach - (count - 1), [1] * (count - 1)
    while surplus > 0:
        movable = [i for i in range(count - 1) if given[i] < reach]
        whole, budget = sum([portions[i] for i in movable]), surplus
        for i in movable:
            extra = min(reach - given[i], max(1, budget * portions[i] // whole), surplus)
            given[i] = given[i] + extra
            surplus = surplus - extra
    return np.array([reach] + given)


def ragged(own_key, amount, total, bound, slope):
    if amount == 2:
        one = jax.random.randint(own_key, (), max(1, total - bound), min(bound, total - 1) + 1)
        return jnp.stack([one, total - one])
    sizes = jnp.asarray(split_up(amount, total, bound, slope), jnp.int32)
    twos = (amount - 1) // 2
    giver, taker = sizes[1:1 + 2 * twos:2], sizes[2:2 + 2 * twos:2]
    room = jnp.minimum(giver - 1, bound - taker)
    passed = jax.random.randint(jax.random.fold_in(own_key, 1), (twos,), 0, 1 << 20) % (room + 1)
    sizes = sizes.at[1:1 + 2 * twos:2].set(giver - passed).at[2:2 + 2 * twos:2].set(taker + passed)
    return sizes[jax.random.permutation(jax.random.fold_in(own_key, 2), amount)]


def scatter_about(own_key, dims, spread, bound, shards=(), dtype=jnp.bfloat16):
    gain = level_of(own_key, dims, shards, -0.22, 0.18) if shards else 1.0
    result = jax.random.normal(own_key, dims, jnp.float32) * spread * gain
    return jnp.minimum(jnp.maximum(result, -bound), bound).astype(dtype)


def setup_inputs(seed: int = 0) -> dict:
    key_of = jax.random.split(jax.random.key(seed), 5)
    inputs = scatter_about(key_of[0], (TOKENS, D), 1.0, 6.0, ((0, 32),))
    segment_ids = jax.vmap(lambda own: jnp.searchsorted(jnp.cumsum(ragged(own, 8, SEQ, SEQ // 4, 1)), jnp.arange(SEQ), side="right"))(jax.random.split(key_of[1], SEQS)).reshape((SEQS, SEQ)).astype(jnp.int32)
    qkv_weight = scatter_about(key_of[2], (D, COLS), D ** -0.5, 0.0625, ((0, 4),))
    attn_cotangent = scatter_about(key_of[3], (TOKENS, QH * HD), 1.0, 6.0, ((0, 32),))
    return dict(inputs=inputs, segment_ids=segment_ids, qkv_weight=qkv_weight, attn_cotangent=attn_cotangent)


def attention_grad(projected, cotangent, segments):
    count = projected.shape[0]
    heads = cotangent.shape[1] // HD
    values = projected.astype(jnp.float32)
    query = values[:, :heads * HD].reshape(count, heads, HD)
    keys = values[:, heads * HD:(heads + 1) * HD]
    vals = values[:, (heads + 1) * HD:]
    positions = jnp.arange(count)
    allowed = (positions[:, None] >= positions[None, :]) & (segments[:, None] == segments[None, :])

    def forward(query, keys, vals):
        scores = jnp.einsum('shd,td->hst', query, keys) / math.sqrt(HD)
        scores = jnp.where(allowed[None], scores, 0.0)
        weights = jnp.where(allowed[None], jnp.exp(scores), 0.0)
        weights = weights / lax.optimization_barrier(jnp.sum(weights, axis=2, keepdims=True))
        return jnp.einsum('hst,td->shd', weights, vals).reshape(count, heads * HD)
    unused, pullback = jax.vjp(forward, query, keys, vals)
    grad_q, grad_k, grad_v = pullback(cotangent.astype(jnp.float32))
    return jnp.concatenate([grad_q.reshape(count, heads * HD), grad_k, grad_v], axis=1).astype(jnp.bfloat16)

def reference(inputs, segment_ids, qkv_weight, attn_cotangent):
    per_group = N_INNER * SEQ
    block_width = D // N_INNER
    weight_blocks = qkv_weight.reshape(N_INNER, block_width, COLS)

    def one_group(packed):
        block_x, block_seg, block_cot = packed
        x_blocks = jnp.transpose(block_x.reshape(per_group, N_INNER, block_width), (1, 0, 2))

        def add_block(total, pair):
            part = jnp.dot(pair[0], pair[1], preferred_element_type=jnp.float32).astype(jnp.bfloat16)
            part = lax.optimization_barrier(part)
            return (total + part.astype(jnp.float32), None)
        summed, unused = lax.scan(add_block, jnp.zeros((per_group, COLS), jnp.float32), (x_blocks, weight_blocks))
        projected = summed.astype(jnp.bfloat16)
        grads = jax.vmap(attention_grad)(projected.reshape(N_INNER, SEQ, COLS), block_cot.reshape(N_INNER, SEQ, QH * HD), block_seg)
        grads = grads.reshape(per_group, COLS)
        input_part = jnp.dot(grads, qkv_weight.T, preferred_element_type=jnp.float32).astype(jnp.bfloat16)
        weight_part = jnp.dot(block_x.T, grads, preferred_element_type=jnp.float32).astype(jnp.bfloat16)
        return (input_part, weight_part)
    input_grad, group_grad = lax.map(one_group, (inputs.reshape(N_OUTER, per_group, D), segment_ids.reshape(N_OUTER, N_INNER, SEQ), attn_cotangent.reshape(N_OUTER, per_group, QH * HD)))
    weight_grad = lax.optimization_barrier(jnp.sum(group_grad.astype(jnp.float32), axis=0))
    return (input_grad.reshape(TOKENS, D), weight_grad)
```

```python
import functools
import math

import jax
import jax.numpy as jnp
from jax import lax
from jax.experimental import pallas as pl
from jax.experimental.pallas import tpu as pltpu
from jax.sharding import PartitionSpec as P

HD = 128
CHUNKS = 4
MESH = pl.DeviceIdType.MESH


def contract(a, b, dims):
    return lax.dot_general(a, b, ((dims[:1], dims[1:]), ((), ())), preferred_element_type=jnp.float32)


def attention_grad(projected, cotangent, seg_row, seg_col):
    count = projected.shape[0]
    heads = cotangent.shape[1] // HD
    query = jnp.concatenate([projected[:, h * HD : (h + 1) * HD] for h in range(heads)], axis=0)
    keys = projected[:, heads * HD : (heads + 1) * HD]
    vals = projected[:, (heads + 1) * HD :]
    cot = jnp.concatenate([cotangent[:, h * HD : (h + 1) * HD] for h in range(heads)], axis=0)
    later = lax.broadcasted_iota(jnp.int32, (count, count), 0)
    earlier = lax.broadcasted_iota(jnp.int32, (count, count), 1)
    bias = jnp.where((later >= earlier) & (seg_col == seg_row), 0.0, -1e30)
    bias = jnp.concatenate([bias] * heads, axis=0)
    scale = 1.0 / math.sqrt(HD)
    scores = contract(query, keys, (1, 1)) * scale + bias
    weights = jnp.exp(scores - jnp.max(scores, axis=1, keepdims=True))
    weights = weights / jnp.sum(weights, axis=1, keepdims=True)
    grad_v = contract(weights.astype(jnp.bfloat16), cot, (0, 0))
    grad_w = contract(cot, vals, (1, 1))
    grad_s = weights * (grad_w - jnp.sum(weights * grad_w, axis=1, keepdims=True)) * scale
    grad_s = grad_s.astype(jnp.bfloat16)
    grad_q = contract(grad_s, keys, (1, 0))
    grad_k = contract(grad_s, query, (0, 0))
    parts = [grad_q[h * count : (h + 1) * count] for h in range(heads)]
    return jnp.concatenate(parts + [grad_k, grad_v], axis=1)


def kernel(
    n, n_outer, halves, x_ref, w_ref, cot_ref, row_ref, col_ref, out_ref, wg_ref,
    w_all, cols, acc, grads, gt_all, rs, got,
    copy_sem, z_send, z_recv, p_send, p_recv, a_send, a_recv, g_send, g_recv, r_send, r_recv,
):
    me = lax.axis_index("inner")
    o = lax.axis_index("outer")
    bits = n_outer.bit_length() - 1
    tok = x_ref.shape[0]
    bw, width = w_ref.shape
    wide = bw // CHUNKS
    part = bw // halves
    piece = part // n_outer
    tile = min(512, bw)

    def bit(b):
        return (o // (1 << b)) % 2

    def across(b):
        return o + (1 - 2 * bit(b)) * (1 << b)

    started = []

    def send(cond, src, dst, s_sem, r_sem, device):
        def make():
            return pltpu.make_async_remote_copy(
                src_ref=src, dst_ref=dst, send_sem=s_sem, recv_sem=r_sem,
                device_id=device, device_id_type=MESH,
            )

        started.append((cond, make))
        if cond is None:
            make().start()
        else:
            @pl.when(cond)
            def _():
                make().start()

    def arrived(dst, r_sem):
        pltpu.make_async_remote_copy(
            src_ref=dst, dst_ref=dst, send_sem=r_sem, recv_sem=r_sem,
            device_id={"inner": (me + 1) % n}, device_id_type=MESH,
        ).wait_recv()

    own = pltpu.make_async_copy(w_ref, w_all.at[pl.ds(pl.multiple_of(me * bw, bw), bw)], copy_sem)
    own.start()

    barrier = pltpu.get_barrier_semaphore()
    for t in range(1, n):
        pl.semaphore_signal(barrier, inc=1, device_id={"inner": (me + t) % n}, device_id_type=MESH)
    for b in range(bits):
        pl.semaphore_signal(barrier, inc=1, device_id={"outer": across(b)}, device_id_type=MESH)
    pl.semaphore_wait(barrier, n - 1 + bits)

    near = jnp.minimum(me, n - 1 - me)
    far_sign = jnp.where(2 * me < n - 1, 1, -1)

    def nth(t):
        sign = -1 if t % 2 else 1
        return jnp.where(t <= 2 * near, me + sign * ((t + 1) // 2), me + far_sign * (t - near))

    def onward(j):
        after = jnp.where(j < me, me + 1, me - 1)
        way = jnp.where(j < me, 0, 1)
        return (after >= 0) & (after < n), jnp.clip(after, 0, n - 1), way

    middle = list(range(1, bits))
    orders = [middle + [0], middle[::-1] + [0]]

    def place(h):
        return sum(bit(b) * (1 << k) for k, b in enumerate(orders[h]))

    def shares(j, h, first, count):
        start = j * bw + h * part + first * piece
        return w_all.at[pl.ds(pl.multiple_of(start, piece), count * piece)]

    def z_start(j, cond, target, way):
        for h in range(halves):
            ref = shares(j, h, place(h), 1)
            send(cond, ref, ref, z_send.at[h, way, j], z_recv.at[h, j], {"inner": target})

    def plane_start(j, k):
        for h in range(halves):
            group = 1 << k
            ref = shares(j, h, place(h) // group * group, group)
            send(None, ref, ref, p_send.at[h, k, j], p_recv.at[h, k, j], {"outer": across(orders[h][k])})

    def plane_wait(j, k):
        for h in range(halves):
            group = 1 << k
            first = place(h) // group * group
            other = first + (1 - 2 * bit(orders[h][k])) * group
            arrived(shares(j, h, other, group), p_recv.at[h, k, j])

    def a2a_start(f):
        for t in range(1, n):
            j = (me + t) % n
            src = x_ref.at[:, pl.ds(pl.multiple_of(j * bw + f * wide, 128), wide)]
            dst = cols.at[pl.ds(pl.multiple_of(me * tok, tok), tok), pl.ds(f * wide, wide)]
            send(None, src, dst, a_send.at[f, j], a_recv.at[f, me], {"inner": j})

    def project(j):
        def body(i, carry):
            start = pl.multiple_of(j * bw + i * tile, tile)
            acc[...] += contract(x_ref[:, pl.ds(start, tile)], w_all[pl.ds(start, tile), :], (1, 0))
            return carry

        lax.fori_loop(0, bw // tile, body, 0)

    own.wait()
    z_start(me, me < n - 1, jnp.minimum(me + 1, n - 1), 0)
    z_start(me, me > 0, jnp.maximum(me - 1, 0), 1)
    acc[...] = jnp.zeros_like(acc)
    project(me)
    cols[pl.ds(pl.multiple_of(me * tok, tok), tok), :] = x_ref[:, pl.ds(pl.multiple_of(me * bw, bw), bw)]

    for turn in range(n - 1 + bits):
        for k in range(bits + 1):
            t = turn - k + 1
            if not 1 <= t <= n - 1:
                continue
            j = nth(t)
            if k == 0:
                for h in range(halves):
                    arrived(shares(j, h, place(h), 1), z_recv.at[h, j])
                cond, target, way = onward(j)
                z_start(j, cond, target, way)
            else:
                plane_wait(j, k - 1)
            if k < bits:
                plane_start(j, k)
            else:
                project(j)
        if turn == n - 3:
            a2a_start(0)
        if turn == n - 2:
            for f in range(1 if n >= 3 else 0, CHUNKS):
                a2a_start(f)

    grad = attention_grad(acc[...].astype(jnp.bfloat16), cot_ref[...], row_ref[...], col_ref[...])
    grads[...] = grad.astype(jnp.bfloat16)

    def gt_part(j):
        return gt_all.at[:, pl.ds(pl.multiple_of(j * tok, tok), tok)]

    def g_start(j, cond, target, way):
        send(cond, gt_part(j), gt_part(j), g_send.at[way, j], g_recv.at[j], {"inner": target})

    gt_all[:, pl.ds(pl.multiple_of(me * tok, tok), tok)] = jnp.transpose(grad).astype(jnp.bfloat16)
    g_start(me, me < n - 1, jnp.minimum(me + 1, n - 1), 0)
    g_start(me, me > 0, jnp.maximum(me - 1, 0), 1)

    def input_part(j):
        def body(i, carry):
            start = pl.multiple_of(j * bw + i * tile, tile)
            out_ref[:, pl.ds(start, tile)] = contract(
                grads[...], w_all[pl.ds(start, tile), :], (1, 1)
            ).astype(out_ref.dtype)
            return carry

        lax.fori_loop(0, bw // tile, body, 0)

    for t in range(1, n):
        input_part(nth(t))
        j = nth(t)
        arrived(gt_part(j), g_recv.at[j])
        cond, target, way = onward(j)
        g_start(j, cond, target, way)
    input_part(me)

    rows = width // n_outer

    def rs_order(f):
        return [0] + (middle if f % 2 == 0 else middle[::-1])

    def rs_region(f, k):
        base = 0
        order = rs_order(f)
        for i in range(k):
            base = base + bit(order[i]) * (width >> (i + 1))
        half = width >> (k + 1)
        b = bit(order[k])
        return base + b * half, base + (1 - b) * half, half

    def got_at(f, k, half):
        return got.at[f, pl.ds(width - (width >> k), half)]

    def rs_start(f, k):
        keep, give, half = rs_region(f, k)
        src = rs.at[f, pl.ds(pl.multiple_of(give, rows), half)]
        send(None, src, got_at(f, k, half), r_send.at[f, k], r_recv.at[f, k], {"outer": across(rs_order(f)[k])})

    def rs_add(f, k):
        keep, give, half = rs_region(f, k)
        arrived(got_at(f, k, half), r_recv.at[f, k])
        at = pl.ds(pl.multiple_of(keep, rows), half)
        total = rs[f, at, :].astype(jnp.float32) + got[f, pl.ds(width - (width >> k), half), :].astype(jnp.float32)
        if k == bits - 1:
            wg_ref[:, f * wide : (f + 1) * wide] = total
        else:
            rs[f, at, :] = total.astype(rs.dtype)

    def weight_part(f):
        for t in range(1, n):
            j = (me + t) % n
            arrived(
                cols.at[pl.ds(pl.multiple_of(j * tok, tok), tok), pl.ds(f * wide, wide)], a_recv.at[f, j]
            )
        order = rs_order(f)
        step = min(256, wide)
        for c in range(wide // step):
            product = contract(gt_all[...], cols[:, f * wide + c * step : f * wide + (c + 1) * step], (1, 0))
            for g in range(n_outer):
                spot = sum(((g >> b) & 1) << (bits - 1 - k) for k, b in enumerate(order))
                rs[f, spot * rows : (spot + 1) * rows, c * step : (c + 1) * step] = product[
                    g * rows : (g + 1) * rows
                ].astype(rs.dtype)

    for turn in range(CHUNKS + bits):
        for k in reversed(range(bits + 1)):
            f = turn - k
            if not 0 <= f < CHUNKS:
                continue
            if k == 0:
                weight_part(f)
            else:
                rs_add(f, k - 1)
            if k < bits:
                rs_start(f, k)

    for cond, make in started:
        if cond is None:
            make().wait_send()
        else:
            @pl.when(cond)
            def _():
                make().wait_send()


def on_device(n, n_outer, inputs, segment_ids, qkv_weight, attn_cotangent):
    tok, depth = inputs.shape
    bw, width = qkv_weight.shape
    bits = n_outer.bit_length() - 1
    halves = 2 if bw % (32 * n_outer) == 0 else 1
    rows = width // n_outer
    wire = jnp.bfloat16 if rows % 16 == 0 else jnp.float32
    wide = bw // CHUNKS
    vmem = pl.BlockSpec(memory_space=pltpu.VMEM)
    dma = pltpu.SemaphoreType.DMA
    input_grad, weight_grad = pl.pallas_call(
        functools.partial(kernel, n, n_outer, halves),
        out_shape=(
            jax.ShapeDtypeStruct((tok, depth), jnp.bfloat16),
            jax.ShapeDtypeStruct((rows, bw), jnp.float32),
        ),
        in_specs=[vmem, pl.BlockSpec(memory_space=pl.ANY), vmem, vmem, vmem],
        out_specs=(vmem, vmem),
        scratch_shapes=[
            pltpu.VMEM((depth, width), jnp.bfloat16),
            pltpu.VMEM((n * tok, bw), jnp.bfloat16),
            pltpu.VMEM((tok, width), jnp.float32),
            pltpu.VMEM((tok, width), jnp.bfloat16),
            pltpu.VMEM((width, n * tok), jnp.bfloat16),
            pltpu.VMEM((CHUNKS, width, wide), wire),
            pltpu.VMEM((CHUNKS, width, wide), wire),
            dma(()),
            dma((halves, 2, n)),
            dma((halves, n)),
            dma((halves, bits, n)),
            dma((halves, bits, n)),
            dma((CHUNKS, n)),
            dma((CHUNKS, n)),
            dma((2, n)),
            dma((n,)),
            dma((CHUNKS, bits)),
            dma((CHUNKS, bits)),
        ],
        compiler_params=pltpu.CompilerParams(
            collective_id=0, has_side_effects=True, vmem_limit_bytes=50 * 1024 * 1024
        ),
        cost_estimate=pl.CostEstimate(
            flops=6 * tok * depth * width, bytes_accessed=12 * tok * depth, transcendentals=0
        ),
    )(inputs, qkv_weight, attn_cotangent, segment_ids.reshape(1, tok), segment_ids.reshape(tok, 1))
    return input_grad, weight_grad.T


def solution(mesh):
    return jax.shard_map(
        functools.partial(on_device, mesh.shape["inner"], mesh.shape["outer"]),
        mesh=mesh,
        in_specs=(
            P(("outer", "inner"), None),
            P(("outer", "inner"), None),
            P("inner", None),
            P(("outer", "inner"), None),
        ),
        out_specs=(P(("outer", "inner"), None), P("inner", "outer")),
        check_vma=False,
    )
```

```python
import functools
import math

import jax
import jax.numpy as jnp
from jax import lax
from jax.experimental import pallas as pl
from jax.experimental.pallas import tpu as pltpu
from jax.sharding import PartitionSpec as P

HD = 128
LAG = 2
MESH = pl.DeviceIdType.MESH


def contract(a, b, dims):
    return lax.dot_general(a, b, ((dims[:1], dims[1:]), ((), ())), preferred_element_type=jnp.float32)


def attention_grad(projected, cotangent, seg_row):
    count = projected.shape[0]
    heads = cotangent.shape[1] // HD
    query = jnp.concatenate([projected[:, h * HD : (h + 1) * HD] for h in range(heads)], axis=0)
    keys = projected[:, heads * HD : (heads + 1) * HD]
    vals = projected[:, (heads + 1) * HD :]
    cot = jnp.concatenate([cotangent[:, h * HD : (h + 1) * HD] for h in range(heads)], axis=0)
    seg_row = jnp.broadcast_to(seg_row.astype(jnp.float32), (count, count))
    seg_col = jnp.transpose(seg_row)
    later = lax.broadcasted_iota(jnp.int32, (count, count), 0)
    earlier = lax.broadcasted_iota(jnp.int32, (count, count), 1)
    bias = jnp.where((later >= earlier) & (seg_col == seg_row), 0.0, -1e30)
    bias = jnp.concatenate([bias] * heads, axis=0)
    scale = 1.0 / math.sqrt(HD)
    scores = contract(query, keys, (1, 1)) * scale + bias
    weights = jnp.exp(scores - jnp.max(scores, axis=1, keepdims=True))
    weights = weights / jnp.sum(weights, axis=1, keepdims=True)
    grad_v = contract(weights.astype(jnp.bfloat16), cot, (0, 0))
    grad_w = contract(cot, vals, (1, 1))
    grad_s = weights * (grad_w - jnp.sum(weights * grad_w, axis=1, keepdims=True)) * scale
    grad_s = grad_s.astype(jnp.bfloat16)
    grad_q = contract(grad_s, keys, (1, 0))
    grad_k = contract(grad_s, query, (0, 0))
    parts = [grad_q[h * count : (h + 1) * count] for h in range(heads)]
    return jnp.concatenate(parts + [grad_k, grad_v], axis=1)


def kernel(
    n, n_outer, halves, wide, x_hbm, w_ref, cot_ref, row_ref, out_ref, wg_ref,
    x_ref, w_all, both, acc, grads, gt, rs, got, fin, fin_got,
    copy_sem, z_send, z_recv, p_send, p_recv, s_send, s_recv, g_send, g_recv, r_send, r_recv, f_send, f_recv,
):
    me = lax.axis_index("inner")
    o = lax.axis_index("outer")
    bits = n_outer.bit_length() - 1
    tok = x_ref.shape[0]
    bw, width = w_ref.shape
    part = bw // halves
    piece = part // n_outer
    tile = min(512, bw)
    pairs = n // 2
    chunks = bw // wide
    parity = me % 2
    mate = me + 1 - 2 * parity

    def bit(b):
        return (o // (1 << b)) % 2

    def across(b):
        return o + (1 - 2 * bit(b)) * (1 << b)

    started = []

    def send(cond, src, dst, s_sem, r_sem, device):
        def make():
            return pltpu.make_async_remote_copy(
                src_ref=src, dst_ref=dst, send_sem=s_sem, recv_sem=r_sem,
                device_id=device, device_id_type=MESH,
            )

        started.append((cond, make))
        if cond is None:
            make().start()
        else:
            @pl.when(cond)
            def _():
                make().start()

    def arrived(dst, r_sem):
        pltpu.make_async_remote_copy(
            src_ref=dst, dst_ref=dst, send_sem=r_sem, recv_sem=r_sem,
            device_id={"inner": (me + 1) % n}, device_id_type=MESH,
        ).wait_recv()

    own = pltpu.make_async_copy(w_ref, w_all.at[pl.ds(pl.multiple_of(me * bw, bw), bw)], copy_sem.at[0])
    own.start()
    fetch = pltpu.make_async_copy(x_hbm, x_ref, copy_sem.at[1])
    fetch.start()

    barrier = pltpu.get_barrier_semaphore()
    for t in range(1, n):
        pl.semaphore_signal(barrier, inc=1, device_id={"inner": (me + t) % n}, device_id_type=MESH)
    for b in range(bits):
        pl.semaphore_signal(barrier, inc=1, device_id={"outer": across(b)}, device_id_type=MESH)
    pl.semaphore_wait(barrier, n - 1 + bits)

    near = jnp.minimum(me, n - 1 - me)
    far_sign = jnp.where(2 * me < n - 1, 1, -1)

    def nth(t):
        sign = -1 if t % 2 else 1
        return jnp.where(t <= 2 * near, me + sign * ((t + 1) // 2), me + far_sign * (t - near))

    def onward(j):
        after = jnp.where(j < me, me + 1, me - 1)
        way = jnp.where(j < me, 0, 1)
        return (after >= 0) & (after < n), jnp.clip(after, 0, n - 1), way

    middle = list(range(1, bits))
    orders = [middle + [0], middle[::-1] + [0]]

    def place(h):
        return sum(bit(b) * (1 << k) for k, b in enumerate(orders[h]))

    def shares(j, h, first, count):
        start = j * bw + h * part + first * piece
        return w_all.at[pl.ds(pl.multiple_of(start, piece), count * piece)]

    def z_start(j, cond, target, way):
        for h in range(halves):
            ref = shares(j, h, place(h), 1)
            send(cond, ref, ref, z_send.at[h, way, j], z_recv.at[h, j], {"inner": target})

    def plane_start(j, k):
        for h in range(halves):
            group = 1 << k
            ref = shares(j, h, place(h) // group * group, group)
            send(None, ref, ref, p_send.at[h, k, j], p_recv.at[h, k, j], {"outer": across(orders[h][k])})

    def plane_wait(j, k, h):
        group = 1 << k
        first = place(h) // group * group
        other = first + (1 - 2 * bit(orders[h][k])) * group
        arrived(shares(j, h, other, group), p_recv.at[h, k, j])

    def swap_start(i):
        src = x_ref.at[:, pl.ds(pl.multiple_of((2 * i + 1 - parity) * bw, bw), bw)]
        dst = both.at[pl.ds(tok, tok), pl.ds(i * bw, bw)]
        send(None, src, dst, s_send.at[i], s_recv.at[i], {"inner": mate})

    def project(j):
        def body(i, carry):
            start = pl.multiple_of(j * bw + i * tile, tile)
            acc[...] += contract(x_ref[:, pl.ds(start, tile)], w_all[pl.ds(start, tile), :], (1, 0))
            return carry

        lax.fori_loop(0, bw // tile, body, 0)

    own.wait()
    z_start(me, me < n - 1, jnp.minimum(me + 1, n - 1), 0)
    z_start(me, me > 0, jnp.maximum(me - 1, 0), 1)
    fetch.wait()
    acc[...] = jnp.zeros_like(acc)
    project(me)
    for i in range(pairs):
        both[:tok, i * bw : (i + 1) * bw] = x_ref[:, pl.ds(pl.multiple_of((2 * i + parity) * bw, bw), bw)]

    events = [(8 * t, t, 0) for t in range(1, n)]
    for t in range(1, n):
        for k in range(bits):
            late = 4 * (2 ** (k + 1) - 2) if k < bits - 1 else 4 * (2**k - 2) + 3
            events.append((12 * t + late, t, k + 1))
    swaps = list(range(pairs))
    for _, t, stage in sorted(events):
        j = nth(t)
        if stage == 0:
            for h in range(halves):
                arrived(shares(j, h, place(h), 1), z_recv.at[h, j])
            cond, target, way = onward(j)
            z_start(j, cond, target, way)
        else:
            for h in range(halves):
                plane_wait(j, stage - 1, h)
        if stage < bits:
            plane_start(j, stage)
        else:
            project(j)
        if stage == 0 and t >= min(2, n - 1):
            for i in swaps if t == n - 1 else swaps[:1]:
                swap_start(i)
            swaps = swaps[1:]

    grad = attention_grad(acc[...].astype(jnp.bfloat16), cot_ref[...], row_ref[...])
    gt[:, :tok] = jnp.transpose(grad).astype(jnp.bfloat16)
    send(None, gt.at[:, pl.ds(0, tok)], gt.at[:, pl.ds(tok, tok)], g_send, g_recv, {"inner": mate})
    grads[...] = grad.astype(jnp.bfloat16)

    def input_part(j):
        def body(i, carry):
            start = pl.multiple_of(j * bw + i * tile, tile)
            out_ref[:, pl.ds(start, tile)] = contract(
                grads[...], w_all[pl.ds(start, tile), :], (1, 1)
            ).astype(out_ref.dtype)
            return carry

        lax.fori_loop(0, bw // tile, body, 0)

    rows = width // n_outer
    units = pairs * chunks

    def pair_of(f):
        return (me // 2 + 1 + f // chunks) % pairs

    def rs_order(f):
        return [0] + (middle if f % 2 == 0 else middle[::-1])

    def rs_region(f, k):
        base = 0
        order = rs_order(f)
        for i in range(k):
            base = base + bit(order[i]) * (width >> (i + 1))
        half = width >> (k + 1)
        b = bit(order[k])
        return base + b * half, base + (1 - b) * half, half

    def got_at(f, k, half):
        return got.at[f, pl.ds(width - (width >> k), half)]

    def rs_start(f, k):
        keep, give, half = rs_region(f, k)
        src = rs.at[f, pl.ds(pl.multiple_of(give, rows), half)]
        send(None, src, got_at(f, k, half), r_send.at[f, k], r_recv.at[f, k], {"outer": across(rs_order(f)[k])})

    def rs_add(f, k):
        keep, give, half = rs_region(f, k)
        arrived(got_at(f, k, half), r_recv.at[f, k])
        at = pl.ds(pl.multiple_of(keep, rows), half)
        total = rs[f, at, :].astype(jnp.float32) + got[f, pl.ds(width - (width >> k), half), :].astype(jnp.float32)
        if k < bits - 1:
            rs[f, at, :] = total.astype(rs.dtype)
            return
        turn, c = f // chunks, f % chunks
        if turn < pairs - 1:
            fin[f] = total.astype(fin.dtype)
            owner = 2 * pair_of(f) + parity
            send(None, fin.at[f], fin_got.at[f], f_send.at[f], f_recv.at[f], {"inner": owner})
        else:
            for other in range(pairs - 1):
                slot = other * chunks + c
                arrived(fin_got.at[slot], f_recv.at[slot])
                total += fin_got[slot].astype(jnp.float32)
            wg_ref[:, c * wide : (c + 1) * wide] = total

    def weight_part(f):
        if f == 0:
            arrived(gt.at[:, pl.ds(tok, tok)], g_recv)
            for i in range(pairs):
                arrived(both.at[pl.ds(tok, tok), pl.ds(i * bw, bw)], s_recv.at[i])
        order = rs_order(f)
        start = pl.multiple_of(pair_of(f) * bw + (f % chunks) * wide, 128)
        product = contract(gt[...], both[:, pl.ds(start, wide)], (1, 0))
        for g in range(n_outer):
            spot = sum(((g >> b) & 1) << (bits - 1 - k) for k, b in enumerate(order))
            rs[f, spot * rows : (spot + 1) * rows, :] = product[g * rows : (g + 1) * rows].astype(rs.dtype)

    blocks = list(range(n))
    input_part(blocks.pop())
    for turn in range(units // 2 + LAG * bits):
        for k in reversed(range(bits + 1)):
            for f in (2 * (turn - LAG * k), 2 * (turn - LAG * k) + 1):
                if not 0 <= f < units:
                    continue
                if k == 0:
                    weight_part(f)
                else:
                    rs_add(f, k - 1)
                if k < bits:
                    rs_start(f, k)
        if blocks and turn >= 1:
            input_part(blocks.pop())
    for j in blocks:
        input_part(j)

    for cond, make in started:
        if cond is None:
            make().wait_send()
        else:
            @pl.when(cond)
            def _():
                make().wait_send()


def on_device(n, n_outer, inputs, segment_ids, qkv_weight, attn_cotangent):
    tok, depth = inputs.shape
    bw, width = qkv_weight.shape
    bits = n_outer.bit_length() - 1
    halves = 2 if bw % (32 * n_outer) == 0 else 1
    rows = width // n_outer
    wire = jnp.bfloat16 if rows % 16 == 0 else jnp.float32
    wide = min(256, bw // 2)
    pairs = n // 2
    units = pairs * bw // wide
    vmem = pl.BlockSpec(memory_space=pltpu.VMEM)
    anywhere = pl.BlockSpec(memory_space=pl.ANY)
    dma = pltpu.SemaphoreType.DMA
    input_grad, weight_grad = pl.pallas_call(
        functools.partial(kernel, n, n_outer, halves, wide),
        out_shape=(
            jax.ShapeDtypeStruct((tok, depth), jnp.bfloat16),
            jax.ShapeDtypeStruct((rows, bw), jnp.float32),
        ),
        in_specs=[anywhere, anywhere, vmem, vmem],
        out_specs=(vmem, vmem),
        scratch_shapes=[
            pltpu.VMEM((tok, depth), jnp.bfloat16),
            pltpu.VMEM((depth, width), jnp.bfloat16),
            pltpu.VMEM((2 * tok, pairs * bw), jnp.bfloat16),
            pltpu.VMEM((tok, width), jnp.float32),
            pltpu.VMEM((tok, width), jnp.bfloat16),
            pltpu.VMEM((width, 2 * tok), jnp.bfloat16),
            pltpu.VMEM((units, width, wide), wire),
            pltpu.VMEM((units, width, wide), wire),
            pltpu.VMEM((units, rows, wide), wire),
            pltpu.VMEM((units, rows, wide), wire),
            dma((2,)),
            dma((halves, 2, n)),
            dma((halves, n)),
            dma((halves, bits, n)),
            dma((halves, bits, n)),
            dma((pairs,)),
            dma((pairs,)),
            dma(()),
            dma(()),
            dma((units, bits)),
            dma((units, bits)),
            dma((units,)),
            dma((units,)),
        ],
        compiler_params=pltpu.CompilerParams(
            collective_id=0, has_side_effects=True, vmem_limit_bytes=54 * 1024 * 1024
        ),
        cost_estimate=pl.CostEstimate(
            flops=6 * tok * depth * width, bytes_accessed=12 * tok * depth, transcendentals=0
        ),
    )(inputs, qkv_weight, attn_cotangent, segment_ids.reshape(1, tok))
    return input_grad, weight_grad.T


def solution(mesh):
    return jax.shard_map(
        functools.partial(on_device, mesh.shape["inner"], mesh.shape["outer"]),
        mesh=mesh,
        in_specs=(
            P(("outer", "inner"), None),
            P(("outer", "inner"), None),
            P("inner", None),
            P(("outer", "inner"), None),
        ),
        out_specs=(P(("outer", "inner"), None), P("inner", "outer")),
        check_vma=False,
    )
```

```python
import functools
import math

import jax
import jax.numpy as jnp
from jax import lax
from jax.experimental import pallas as pl
from jax.experimental.pallas import tpu as pltpu
from jax.sharding import PartitionSpec as P

HD = 128
LAG = 2
MESH = pl.DeviceIdType.MESH


def contract(a, b, dims):
    return lax.dot_general(a, b, ((dims[:1], dims[1:]), ((), ())), preferred_element_type=jnp.float32)


def attention_grad(projected, cotangent, seg_row):
    count = projected.shape[0]
    heads = cotangent.shape[1] // HD
    query = jnp.concatenate([projected[:, h * HD : (h + 1) * HD] for h in range(heads)], axis=0)
    keys = projected[:, heads * HD : (heads + 1) * HD]
    vals = projected[:, (heads + 1) * HD :]
    cot = jnp.concatenate([cotangent[:, h * HD : (h + 1) * HD] for h in range(heads)], axis=0)
    seg_row = jnp.broadcast_to(seg_row.astype(jnp.float32), (count, count))
    seg_col = jnp.transpose(seg_row)
    later = lax.broadcasted_iota(jnp.int32, (count, count), 0)
    earlier = lax.broadcasted_iota(jnp.int32, (count, count), 1)
    bias = jnp.where((later >= earlier) & (seg_col == seg_row), 0.0, -1e30)
    bias = jnp.concatenate([bias] * heads, axis=0)
    scale = 1.0 / math.sqrt(HD)
    scores = contract(query, keys, (1, 1)) * scale + bias
    weights = jnp.exp(scores - jnp.max(scores, axis=1, keepdims=True))
    weights = weights / jnp.sum(weights, axis=1, keepdims=True)
    grad_v = contract(weights.astype(jnp.bfloat16), cot, (0, 0))
    grad_w = contract(cot, vals, (1, 1))
    grad_s = weights * (grad_w - jnp.sum(weights * grad_w, axis=1, keepdims=True)) * scale
    grad_s = grad_s.astype(jnp.bfloat16)
    grad_q = contract(grad_s, keys, (1, 0))
    grad_k = contract(grad_s, query, (0, 0))
    parts = [grad_q[h * count : (h + 1) * count] for h in range(heads)]
    return jnp.concatenate(parts + [grad_k, grad_v], axis=1)


def kernel(
    n, n_outer, parts, wide, x_hbm, w_ref, cot_ref, row_ref, out_ref, wg_ref,
    x_ref, w_all, both, acc, mine, theirs, grads, mate_grads, back, gt, rs, got, fin, fin_got,
    copy_sem, z_send, z_recv, p_send, p_recv, s_send, s_recv, q_send, q_recv, g_send, g_recv, b_send, b_recv,
    r_send, r_recv, f_send, f_recv,
):
    me = lax.axis_index("inner")
    o = lax.axis_index("outer")
    bits = n_outer.bit_length() - 1
    tok = x_ref.shape[0]
    bw, width = w_ref.shape
    part = bw // parts
    piece = part // n_outer
    tile = min(512, bw)
    step = min(1024, bw)
    steps = bw // step
    pairs = n // 2
    slot = me // 2
    chunks = bw // wide
    parity = me % 2
    mate = me + 1 - 2 * parity

    def bit(b):
        return (o // (1 << b)) % 2

    def across(b):
        return o + (1 - 2 * bit(b)) * (1 << b)

    started = []

    def send(cond, src, dst, s_sem, r_sem, device):
        def make():
            return pltpu.make_async_remote_copy(
                src_ref=src, dst_ref=dst, send_sem=s_sem, recv_sem=r_sem,
                device_id=device, device_id_type=MESH,
            )

        started.append((cond, make))
        if cond is None:
            make().start()
        else:
            @pl.when(cond)
            def _():
                make().start()

    def arrived(dst, r_sem):
        pltpu.make_async_remote_copy(
            src_ref=dst, dst_ref=dst, send_sem=r_sem, recv_sem=r_sem,
            device_id={"inner": (me + 1) % n}, device_id_type=MESH,
        ).wait_recv()

    own = pltpu.make_async_copy(w_ref, w_all.at[pl.ds(pl.multiple_of(slot * bw, bw), bw)], copy_sem.at[0])
    own.start()
    fetch = pltpu.make_async_copy(x_hbm, x_ref, copy_sem.at[1])
    fetch.start()

    barrier = pltpu.get_barrier_semaphore()
    for t in range(1, n):
        pl.semaphore_signal(barrier, inc=1, device_id={"inner": (me + t) % n}, device_id_type=MESH)
    for b in range(bits):
        pl.semaphore_signal(barrier, inc=1, device_id={"outer": across(b)}, device_id_type=MESH)
    pl.semaphore_wait(barrier, n - 1 + bits)

    def nth(t):
        return (slot + t) % pairs

    def block(i):
        return 2 * i + parity

    middle = list(range(1, bits))
    orders = [middle + [0], middle[::-1] + [0]] * 2
    groups = [[0, 1], [2, 3]] if parts == 4 else [[h] for h in range(parts)]

    def place(h):
        return sum(bit(b) * (1 << k) for k, b in enumerate(orders[h]))

    def shares(i, h, first, count):
        start = i * bw + h * part + first * piece
        return w_all.at[pl.ds(pl.multiple_of(start, piece), count * piece)]

    def z_start(t, h):
        ref = shares(slot, h, place(h), 1)
        send(None, ref, ref, z_send.at[h, nth(t)], z_recv.at[h, slot], {"inner": block(nth(t))})

    def plane_start(i, k, h):
        group = 1 << k
        ref = shares(i, h, place(h) // group * group, group)
        send(None, ref, ref, p_send.at[h, k, i], p_recv.at[h, k, i], {"outer": across(orders[h][k])})

    def plane_wait(i, k, h):
        group = 1 << k
        first = place(h) // group * group
        other = first + (1 - 2 * bit(orders[h][k])) * group
        arrived(shares(i, h, other, group), p_recv.at[h, k, i])

    def both_part(i, c):
        return both.at[pl.ds(tok, tok), pl.ds(pl.multiple_of(i * bw + c * step, step), step)]

    def swap_start(t, c):
        i = nth(t)
        src = x_ref.at[:, pl.ds(pl.multiple_of((2 * i + 1 - parity) * bw + c * step, step), step)]
        send(None, src, both_part(i, c), s_send.at[i, c], s_recv.at[i, c], {"inner": mate})

    def project(t, c):
        i = nth(t)
        arrived(both_part(i, c), s_recv.at[i, c])

        def body(r, carry):
            start = pl.multiple_of(i * bw + c * step + r * tile, tile)
            acc[...] += contract(both[:, pl.ds(start, tile)], w_all[pl.ds(start, tile), :], (1, 0))
            return carry

        lax.fori_loop(0, step // tile, body, 0)

    swaps = [(t, c) for t in range(pairs) for c in range(steps)]

    def swap_some(count):
        for t, c in swaps[:count]:
            swap_start(t, c)
        del swaps[:count]

    own.wait()
    for group in groups:
        for t in range(1, pairs):
            for h in group:
                z_start(t, h)
    fetch.wait()
    swap_some(1)
    acc[...] = jnp.zeros_like(acc)
    for i in range(pairs):
        both[:tok, i * bw : (i + 1) * bw] = x_ref[:, pl.ds(pl.multiple_of(block(i) * bw, bw), bw)]

    trips = [(t, group) for t in range(1, pairs) for group in groups]
    for turn in range(len(trips) + bits):
        for k in reversed(range(bits + 1)):
            if not 0 <= turn - k < len(trips):
                continue
            t, group = trips[turn - k]
            for h in group:
                if k == 0:
                    arrived(shares(nth(t), h, place(h), 1), z_recv.at[h, nth(t)])
                else:
                    plane_wait(nth(t), k - 1, h)
                if k < bits:
                    plane_start(nth(t), k, h)
        if turn < len(trips):
            swap_some(1 if turn < len(trips) - 1 else len(swaps))
        if turn == len(trips):
            project(0, 0)
    swap_some(len(swaps))
    for t in range(pairs):
        for c in range(steps):
            if (t, c) != (0, 0):
                project(t, c)

    mine[...] = acc[tok:, :].astype(mine.dtype)
    send(None, mine, theirs, q_send, q_recv, {"inner": mate})
    arrived(theirs, q_recv)
    projected = (acc[:tok, :] + theirs[...].astype(jnp.float32)).astype(jnp.bfloat16)
    grad = attention_grad(projected, cot_ref[...], row_ref[...])
    gt[:, :tok] = jnp.transpose(grad).astype(jnp.bfloat16)
    send(None, gt.at[:, pl.ds(0, tok)], gt.at[:, pl.ds(tok, tok)], g_send, g_recv, {"inner": mate})
    grads[...] = grad.astype(jnp.bfloat16)

    def input_part(g_ref, i, c, put):
        def body(r, carry):
            start = c * step + r * tile
            rows_at = pl.ds(pl.multiple_of(i * bw + start, tile), tile)
            put(start, contract(g_ref[...], w_all[rows_at, :], (1, 1)).astype(jnp.bfloat16))
            return carry

        lax.fori_loop(0, step // tile, body, 0)

    def input_own(i, c):
        def put(start, value):
            out_ref[:, pl.ds(pl.multiple_of(block(i) * bw + start, tile), tile)] = value

        input_part(grads, i, c, put)

    def input_mate(i, c):
        def put(start, value):
            back[:, pl.ds(pl.multiple_of(i * bw + start, tile), tile)] = value

        input_part(mate_grads, i, c, put)
        src = back.at[:, pl.ds(i * bw + c * step, step)]
        dst = out_ref.at[:, pl.ds(pl.multiple_of(block(i) * bw + c * step, step), step)]
        send(None, src, dst, b_send.at[i, c], b_recv.at[i, c], {"inner": mate})

    rows = width // n_outer
    units = pairs * chunks

    def pair_of(f):
        return (slot + 1 + f // chunks) % pairs

    def rs_order(f):
        return [0] + (middle if f % 2 == 0 else middle[::-1])

    def rs_region(f, k):
        base = 0
        order = rs_order(f)
        for i in range(k):
            base = base + bit(order[i]) * (width >> (i + 1))
        half = width >> (k + 1)
        b = bit(order[k])
        return base + b * half, base + (1 - b) * half, half

    def got_at(f, k, half):
        return got.at[f, pl.ds(width - (width >> k), half)]

    def rs_start(f, k):
        keep, give, half = rs_region(f, k)
        src = rs.at[f, pl.ds(pl.multiple_of(give, rows), half)]
        send(None, src, got_at(f, k, half), r_send.at[f, k], r_recv.at[f, k], {"outer": across(rs_order(f)[k])})

    def rs_add(f, k):
        keep, give, half = rs_region(f, k)
        arrived(got_at(f, k, half), r_recv.at[f, k])
        at = pl.ds(pl.multiple_of(keep, rows), half)
        total = rs[f, at, :].astype(jnp.float32) + got[f, pl.ds(width - (width >> k), half), :].astype(jnp.float32)
        if k < bits - 1:
            rs[f, at, :] = total.astype(rs.dtype)
            return
        turn, c = f // chunks, f % chunks
        if turn < pairs - 1:
            fin[f] = total.astype(fin.dtype)
            owner = 2 * pair_of(f) + parity
            send(None, fin.at[f], fin_got.at[f], f_send.at[f], f_recv.at[f], {"inner": owner})
        else:
            for other in range(pairs - 1):
                spot = other * chunks + c
                arrived(fin_got.at[spot], f_recv.at[spot])
                total += fin_got[spot].astype(jnp.float32)
            wg_ref[:, c * wide : (c + 1) * wide] = total

    def weight_part(f):
        if f == 0:
            arrived(gt.at[:, pl.ds(tok, tok)], g_recv)
        order = rs_order(f)
        start = pl.multiple_of(pair_of(f) * bw + (f % chunks) * wide, 128)
        product = contract(gt[...], both[:, pl.ds(start, wide)], (1, 0))
        for g in range(n_outer):
            spot = sum(((g >> b) & 1) << (bits - 1 - k) for k, b in enumerate(order))
            rs[f, spot * rows : (spot + 1) * rows, :] = product[g * rows : (g + 1) * rows].astype(rs.dtype)

    inputs = [(i, c) for i in range(pairs) for c in range(steps)]
    for i, c in inputs:
        input_own(i, c)
    backs = list(inputs)
    for turn in range(units // 2 + LAG * bits):
        for k in reversed(range(bits + 1)):
            for f in (2 * (turn - LAG * k), 2 * (turn - LAG * k) + 1):
                if not 0 <= f < units:
                    continue
                if k == 0:
                    weight_part(f)
                else:
                    rs_add(f, k - 1)
                if k < bits:
                    rs_start(f, k)
        if turn == 0:
            mate_grads[...] = jnp.transpose(gt[:, tok:].astype(jnp.float32)).astype(jnp.bfloat16)
        if backs:
            input_mate(*backs.pop(0))
    for i, c in backs:
        input_mate(i, c)
    for i, c in inputs:
        spot = (2 * i + 1 - parity) * bw + c * step
        arrived(out_ref.at[:, pl.ds(pl.multiple_of(spot, step), step)], b_recv.at[i, c])

    for cond, make in started:
        if cond is None:
            make().wait_send()
        else:
            @pl.when(cond)
            def _():
                make().wait_send()


def on_device(n, n_outer, inputs, segment_ids, qkv_weight, attn_cotangent):
    tok, depth = inputs.shape
    bw, width = qkv_weight.shape
    bits = n_outer.bit_length() - 1
    parts = 4 if bw % (64 * n_outer) == 0 else 1
    steps = bw // min(1024, bw)
    rows = width // n_outer
    wire = jnp.bfloat16 if rows % 16 == 0 else jnp.float32
    wide = min(256, bw // 2)
    pairs = n // 2
    units = pairs * bw // wide
    vmem = pl.BlockSpec(memory_space=pltpu.VMEM)
    anywhere = pl.BlockSpec(memory_space=pl.ANY)
    dma = pltpu.SemaphoreType.DMA
    input_grad, weight_grad = pl.pallas_call(
        functools.partial(kernel, n, n_outer, parts, wide),
        out_shape=(
            jax.ShapeDtypeStruct((tok, depth), jnp.bfloat16),
            jax.ShapeDtypeStruct((rows, bw), jnp.float32),
        ),
        in_specs=[anywhere, anywhere, vmem, vmem],
        out_specs=(vmem, vmem),
        scratch_shapes=[
            pltpu.VMEM((tok, depth), jnp.bfloat16),
            pltpu.VMEM((pairs * bw, width), jnp.bfloat16),
            pltpu.VMEM((2 * tok, pairs * bw), jnp.bfloat16),
            pltpu.VMEM((2 * tok, width), jnp.float32),
            pltpu.VMEM((tok, width), jnp.bfloat16),
            pltpu.VMEM((tok, width), jnp.bfloat16),
            pltpu.VMEM((tok, width), jnp.bfloat16),
            pltpu.VMEM((tok, width), jnp.bfloat16),
            pltpu.VMEM((tok, pairs * bw), jnp.bfloat16),
            pltpu.VMEM((width, 2 * tok), jnp.bfloat16),
            pltpu.VMEM((units, width, wide), wire),
            pltpu.VMEM((units, width, wide), wire),
            pltpu.VMEM((units, rows, wide), wire),
            pltpu.VMEM((units, rows, wide), wire),
            dma((2,)),
            dma((parts, pairs)),
            dma((parts, pairs)),
            dma((parts, bits, pairs)),
            dma((parts, bits, pairs)),
            dma((pairs, steps)),
            dma((pairs, steps)),
            dma(()),
            dma(()),
            dma(()),
            dma(()),
            dma((pairs, steps)),
            dma((pairs, steps)),
            dma((units, bits)),
            dma((units, bits)),
            dma((units,)),
            dma((units,)),
        ],
        compiler_params=pltpu.CompilerParams(
            collective_id=0, has_side_effects=True, vmem_limit_bytes=48 * 1024 * 1024
        ),
        cost_estimate=pl.CostEstimate(
            flops=6 * tok * depth * width, bytes_accessed=12 * tok * depth, transcendentals=0
        ),
    )(inputs, qkv_weight, attn_cotangent, segment_ids.reshape(1, tok))
    return input_grad, weight_grad.T


def solution(mesh):
    return jax.shard_map(
        functools.partial(on_device, mesh.shape["inner"], mesh.shape["outer"]),
        mesh=mesh,
        in_specs=(
            P(("outer", "inner"), None),
            P(("outer", "inner"), None),
            P("inner", None),
            P(("outer", "inner"), None),
        ),
        out_specs=(P(("outer", "inner"), None), P("inner", "outer")),
        check_vma=False,
    )
```

```python
import functools
import math

import jax
import jax.numpy as jnp
from jax import lax
from jax.experimental import pallas as pl
from jax.experimental.pallas import tpu as pltpu
from jax.sharding import PartitionSpec as P

HD = 128
LAG = 2
MESH = pl.DeviceIdType.MESH


def contract(a, b, dims):
    return lax.dot_general(a, b, ((dims[:1], dims[1:]), ((), ())), preferred_element_type=jnp.float32)


def allowed_bias(seg_row, heads):
    count = seg_row.shape[1]
    seg_row = jnp.broadcast_to(seg_row.astype(jnp.float32), (count, count))
    seg_col = jnp.transpose(seg_row)
    later = lax.broadcasted_iota(jnp.int32, (count, count), 0)
    earlier = lax.broadcasted_iota(jnp.int32, (count, count), 1)
    bias = jnp.where((later >= earlier) & (seg_col == seg_row), 0.0, -1e30)
    return jnp.concatenate([bias] * heads, axis=0)


def attention_grad(query, keys, vals, cot, bias):
    scale = 1.0 / math.sqrt(HD)
    scores = contract(query, keys, (1, 1)) * scale + bias
    grad_w = contract(cot, vals, (1, 1))
    weights = jnp.exp(scores - jnp.max(scores, axis=1, keepdims=True))
    weights = weights / jnp.sum(weights, axis=1, keepdims=True)
    grad_s = weights * (grad_w - jnp.sum(weights * grad_w, axis=1, keepdims=True)) * scale
    grad_s = grad_s.astype(jnp.bfloat16)
    grad_q = contract(grad_s, keys, (1, 0))
    grad_k = contract(grad_s, query, (0, 0))
    grad_v = contract(weights.astype(jnp.bfloat16), cot, (0, 0))
    return grad_q, grad_k, grad_v


def kernel(
    n, n_outer, parts, wide, x_hbm, w_ref, cot_hbm, row_hbm, out_ref, wg_ref,
    x_ref, cot_ref, row_ref, w_all, both, acc, mine, theirs, grads, mate_grads, ready, back, gt, rs, got, fin, fin_got,
    copy_sem, z_send, z_recv, p_send, p_recv, s_send, s_recv, q_send, q_recv, g_send, g_recv, b_send, b_recv,
    r_send, r_recv, f_send, f_recv, o_sem,
):
    me = lax.axis_index("inner")
    o = lax.axis_index("outer")
    bits = n_outer.bit_length() - 1
    tok = x_ref.shape[0]
    bw, width = w_ref.shape
    part = bw // parts
    piece = part // n_outer
    tile = min(512, bw)
    step = min(1024, bw)
    steps = bw // step
    pairs = n // 2
    slot = me // 2
    chunks = bw // wide
    parity = me % 2
    mate = me + 1 - 2 * parity

    def bit(b):
        return (o // (1 << b)) % 2

    def across(b):
        return o + (1 - 2 * bit(b)) * (1 << b)

    started = []

    def send(cond, src, dst, s_sem, r_sem, device):
        def make():
            return pltpu.make_async_remote_copy(
                src_ref=src, dst_ref=dst, send_sem=s_sem, recv_sem=r_sem,
                device_id=device, device_id_type=MESH,
            )

        started.append((cond, make))
        if cond is None:
            make().start()
        else:
            @pl.when(cond)
            def _():
                make().start()

    def arrived(dst, r_sem):
        pltpu.make_async_remote_copy(
            src_ref=dst, dst_ref=dst, send_sem=r_sem, recv_sem=r_sem,
            device_id={"inner": (me + 1) % n}, device_id_type=MESH,
        ).wait_recv()

    own = pltpu.make_async_copy(w_ref, w_all.at[pl.ds(pl.multiple_of(slot * bw, bw), bw)], copy_sem.at[0])
    own.start()
    fetch = pltpu.make_async_copy(x_hbm, x_ref, copy_sem.at[1])
    fetch.start()
    small = [
        pltpu.make_async_copy(cot_hbm, cot_ref, copy_sem.at[2]),
        pltpu.make_async_copy(row_hbm, row_ref, copy_sem.at[3]),
    ]
    for copy in small:
        copy.start()

    barrier = pltpu.get_barrier_semaphore()
    for t in range(1, n):
        pl.semaphore_signal(barrier, inc=1, device_id={"inner": (me + t) % n}, device_id_type=MESH)
    for b in range(bits):
        pl.semaphore_signal(barrier, inc=1, device_id={"outer": across(b)}, device_id_type=MESH)
    pl.semaphore_wait(barrier, n - 1 + bits)

    def nth(t):
        return (slot + t) % pairs

    def block(i):
        return 2 * i + parity

    middle = list(range(1, bits))
    orders = [middle + [0], middle[::-1] + [0]] * 2
    groups = [[0, 1], [2, 3]] if parts == 4 else [[h] for h in range(parts)]

    def place(h):
        return sum(bit(b) * (1 << k) for k, b in enumerate(orders[h]))

    def shares(i, h, first, count):
        start = i * bw + h * part + first * piece
        return w_all.at[pl.ds(pl.multiple_of(start, piece), count * piece)]

    def z_start(t, h):
        ref = shares(slot, h, place(h), 1)
        send(None, ref, ref, z_send.at[h, nth(t)], z_recv.at[h, slot], {"inner": block(nth(t))})

    def plane_start(i, k, h):
        group = 1 << k
        ref = shares(i, h, place(h) // group * group, group)
        send(None, ref, ref, p_send.at[h, k, i], p_recv.at[h, k, i], {"outer": across(orders[h][k])})

    def plane_wait(i, k, h):
        group = 1 << k
        first = place(h) // group * group
        other = first + (1 - 2 * bit(orders[h][k])) * group
        arrived(shares(i, h, other, group), p_recv.at[h, k, i])

    def both_part(i, c):
        return both.at[pl.ds(tok, tok), pl.ds(pl.multiple_of(i * bw + c * step, step), step)]

    def swap_start(t, c):
        i = nth(t)
        src = x_ref.at[:, pl.ds(pl.multiple_of((2 * i + 1 - parity) * bw + c * step, step), step)]
        send(None, src, both_part(i, c), s_send.at[i, c], s_recv.at[i, c], {"inner": mate})

    def project(t, c):
        i = nth(t)
        arrived(both_part(i, c), s_recv.at[i, c])

        def body(r, carry):
            start = pl.multiple_of(i * bw + c * step + r * tile, tile)
            acc[...] += contract(both[:, pl.ds(start, tile)], w_all[pl.ds(start, tile), :], (1, 0))
            return carry

        lax.fori_loop(0, step // tile, body, 0)

    swaps = [(t, c) for t in range(pairs) for c in range(steps)]

    def swap_some(count):
        for t, c in swaps[:count]:
            swap_start(t, c)
        del swaps[:count]

    own.wait()
    for group in groups:
        for t in range(1, pairs):
            for h in group:
                z_start(t, h)
    fetch.wait()
    swap_some(1)
    for copy in small:
        copy.wait()
    acc[...] = jnp.zeros_like(acc)
    for i in range(pairs):
        both[:tok, i * bw : (i + 1) * bw] = x_ref[:, pl.ds(pl.multiple_of(block(i) * bw, bw), bw)]

    trips = [(t, group) for t in range(1, pairs) for group in groups]
    for turn in range(len(trips) + bits):
        for k in reversed(range(bits + 1)):
            if not 0 <= turn - k < len(trips):
                continue
            t, group = trips[turn - k]
            for h in group:
                if k == 0:
                    arrived(shares(nth(t), h, place(h), 1), z_recv.at[h, nth(t)])
                else:
                    plane_wait(nth(t), k - 1, h)
                if k < bits:
                    plane_start(nth(t), k, h)
        if turn < len(trips):
            swap_some(1 if turn < len(trips) - 1 else len(swaps))
        if turn == len(trips):
            project(0, 0)
    swap_some(len(swaps))
    for t in range(pairs):
        for c in range(steps):
            if (t, c) != (0, 0):
                project(t, c)

    heads = cot_ref.shape[1] // HD
    kv = heads * HD
    lots = [range(h, min(h + 2, heads)) for h in range(0, heads, 2)]
    spans = [(lot[0] * HD, len(lot) * HD) for lot in lots] + [(kv, 2 * HD)]
    last = len(lots)
    for p in [last] + list(range(last)):
        at = pl.ds(spans[p][0], spans[p][1])
        mine[:, at] = acc[tok:, at].astype(mine.dtype)
        send(None, mine.at[:, at], theirs.at[:, at], q_send.at[p], q_recv.at[p], {"inner": mate})

    def projected(p):
        at = pl.ds(spans[p][0], spans[p][1])
        arrived(theirs.at[:, at], q_recv.at[p])
        return (acc[:tok, at] + theirs[:, at].astype(jnp.float32)).astype(jnp.bfloat16)

    def stacked(value):
        return jnp.concatenate([value[:, h : h + HD] for h in range(0, value.shape[1], HD)], axis=0)

    def grads_out(p, value):
        start, size = spans[p]
        gt[start : start + size, :tok] = jnp.transpose(value).astype(jnp.bfloat16)
        at = pl.ds(start, size)
        send(None, gt.at[at, pl.ds(0, tok)], gt.at[at, pl.ds(tok, tok)], g_send.at[p], g_recv.at[p], {"inner": mate})
        grads[:, start : start + size] = value.astype(jnp.bfloat16)

    keys_vals = projected(last)
    keys, vals = keys_vals[:, :HD], keys_vals[:, HD:]
    grad_k, grad_v = 0.0, 0.0
    for p, lot in enumerate(lots):
        bias = allowed_bias(row_ref[...], len(lot))
        cot = stacked(cot_ref[:, lot[0] * HD : (lot[-1] + 1) * HD])
        grad_q, part_k, part_v = attention_grad(stacked(projected(p)), keys, vals, cot, bias)
        grad_k, grad_v = grad_k + part_k, grad_v + part_v
        grads_out(p, jnp.concatenate([grad_q[h * tok : (h + 1) * tok] for h in range(len(lot))], axis=1))
    grads_out(last, jnp.concatenate([grad_k, grad_v], axis=1))

    def input_part(g_ref, i, c, put):
        def body(r, carry):
            start = c * step + r * tile
            rows_at = pl.ds(pl.multiple_of(i * bw + start, tile), tile)
            put(start, contract(g_ref[...], w_all[rows_at, :], (1, 1)).astype(jnp.bfloat16))
            return carry

        lax.fori_loop(0, step // tile, body, 0)

    def input_own(i, c):
        def put(start, value):
            ready[:, pl.ds(pl.multiple_of(i * bw + start, tile), tile)] = value

        input_part(grads, i, c, put)
        write(i, c).start()

    def write(i, c):
        src = ready.at[:, pl.ds(i * bw + c * step, step)]
        dst = out_ref.at[:, pl.ds(pl.multiple_of(block(i) * bw + c * step, step), step)]
        return pltpu.make_async_copy(src, dst, o_sem.at[i, c])

    def input_mate(i, c):
        def put(start, value):
            back[:, pl.ds(pl.multiple_of(i * bw + start, tile), tile)] = value

        input_part(mate_grads, i, c, put)
        src = back.at[:, pl.ds(i * bw + c * step, step)]
        dst = out_ref.at[:, pl.ds(pl.multiple_of(block(i) * bw + c * step, step), step)]
        send(None, src, dst, b_send.at[i, c], b_recv.at[i, c], {"inner": mate})

    rows = width // n_outer
    units = pairs * chunks

    def pair_of(f):
        return (slot + 1 + f // chunks) % pairs

    def rs_order(f):
        return [0] + (middle if f % 2 == 0 else middle[::-1])

    def rs_region(f, k):
        base = 0
        order = rs_order(f)
        for i in range(k):
            base = base + bit(order[i]) * (width >> (i + 1))
        half = width >> (k + 1)
        b = bit(order[k])
        return base + b * half, base + (1 - b) * half, half

    def got_at(f, k, half):
        return got.at[f, pl.ds(width - (width >> k), half)]

    def rs_start(f, k):
        keep, give, half = rs_region(f, k)
        src = rs.at[f, pl.ds(pl.multiple_of(give, rows), half)]
        send(None, src, got_at(f, k, half), r_send.at[f, k], r_recv.at[f, k], {"outer": across(rs_order(f)[k])})

    def rs_add(f, k):
        keep, give, half = rs_region(f, k)
        arrived(got_at(f, k, half), r_recv.at[f, k])
        at = pl.ds(pl.multiple_of(keep, rows), half)
        total = rs[f, at, :].astype(jnp.float32) + got[f, pl.ds(width - (width >> k), half), :].astype(jnp.float32)
        if k < bits - 1:
            rs[f, at, :] = total.astype(rs.dtype)
            return
        turn, c = f // chunks, f % chunks
        if turn < pairs - 1:
            fin[f] = total.astype(fin.dtype)
            owner = 2 * pair_of(f) + parity
            send(None, fin.at[f], fin_got.at[f], f_send.at[f], f_recv.at[f], {"inner": owner})
        else:
            for other in range(pairs - 1):
                spot = other * chunks + c
                arrived(fin_got.at[spot], f_recv.at[spot])
                total += fin_got[spot].astype(jnp.float32)
            wg_ref[:, c * wide : (c + 1) * wide] = total

    def weight_part(f):
        if f == 0:
            for p, (start, size) in enumerate(spans):
                arrived(gt.at[pl.ds(start, size), pl.ds(tok, tok)], g_recv.at[p])
        order = rs_order(f)
        start = pl.multiple_of(pair_of(f) * bw + (f % chunks) * wide, 128)
        product = contract(gt[...], both[:, pl.ds(start, wide)], (1, 0))
        for g in range(n_outer):
            spot = sum(((g >> b) & 1) << (bits - 1 - k) for k, b in enumerate(order))
            rs[f, spot * rows : (spot + 1) * rows, :] = product[g * rows : (g + 1) * rows].astype(rs.dtype)

    inputs = [(i, c) for i in range(pairs) for c in range(steps)]
    for i, c in inputs:
        input_own(i, c)
    backs = list(inputs)
    lags = [0] + [1 + LAG * k for k in range(bits)]
    for turn in range(units // 2 + lags[-1]):
        for k in reversed(range(bits + 1)):
            for f in (2 * (turn - lags[k]), 2 * (turn - lags[k]) + 1):
                if not 0 <= f < units:
                    continue
                if k == 0:
                    weight_part(f)
                else:
                    rs_add(f, k - 1)
                if k < bits:
                    rs_start(f, k)
        if turn == 0:
            mate_grads[...] = jnp.transpose(gt[:, tok:].astype(jnp.float32)).astype(jnp.bfloat16)
        if backs:
            input_mate(*backs.pop(0))
    for i, c in backs:
        input_mate(i, c)
    for i, c in inputs:
        spot = (2 * i + 1 - parity) * bw + c * step
        arrived(out_ref.at[:, pl.ds(pl.multiple_of(spot, step), step)], b_recv.at[i, c])
        write(i, c).wait()

    for cond, make in started:
        if cond is None:
            make().wait_send()
        else:
            @pl.when(cond)
            def _():
                make().wait_send()


def on_device(n, n_outer, inputs, segment_ids, qkv_weight, attn_cotangent):
    tok, depth = inputs.shape
    bw, width = qkv_weight.shape
    bits = n_outer.bit_length() - 1
    parts = 4 if bw % (64 * n_outer) == 0 else 1
    steps = bw // min(1024, bw)
    rows = width // n_outer
    wire = jnp.bfloat16 if rows % 16 == 0 else jnp.float32
    wide = min(256, bw // 2)
    pairs = n // 2
    units = pairs * bw // wide
    vmem = pl.BlockSpec(memory_space=pltpu.VMEM)
    hbm = pl.BlockSpec(memory_space=pltpu.HBM)
    dma = pltpu.SemaphoreType.DMA
    input_grad, weight_grad = pl.pallas_call(
        functools.partial(kernel, n, n_outer, parts, wide),
        out_shape=(
            jax.ShapeDtypeStruct((tok, depth), jnp.bfloat16),
            jax.ShapeDtypeStruct((rows, bw), jnp.float32),
        ),
        in_specs=[hbm] * 4,
        out_specs=(hbm, vmem),
        scratch_shapes=[
            pltpu.VMEM((tok, depth), jnp.bfloat16),
            pltpu.VMEM(attn_cotangent.shape, jnp.bfloat16),
            pltpu.VMEM((1, tok), jnp.int32),
            pltpu.VMEM((pairs * bw, width), jnp.bfloat16),
            pltpu.VMEM((2 * tok, pairs * bw), jnp.bfloat16),
            pltpu.VMEM((2 * tok, width), jnp.float32),
            pltpu.VMEM((tok, width), jnp.bfloat16),
            pltpu.VMEM((tok, width), jnp.bfloat16),
            pltpu.VMEM((tok, width), jnp.bfloat16),
            pltpu.VMEM((tok, width), jnp.bfloat16),
            pltpu.VMEM((tok, pairs * bw), jnp.bfloat16),
            pltpu.VMEM((tok, pairs * bw), jnp.bfloat16),
            pltpu.VMEM((width, 2 * tok), jnp.bfloat16),
            pltpu.VMEM((units, width, wide), wire),
            pltpu.VMEM((units, width, wide), wire),
            pltpu.VMEM((units, rows, wide), wire),
            pltpu.VMEM((units, rows, wide), wire),
            dma((4,)),
            dma((parts, pairs)),
            dma((parts, pairs)),
            dma((parts, bits, pairs)),
            dma((parts, bits, pairs)),
            dma((pairs, steps)),
            dma((pairs, steps)),
            dma((width // HD,)),
            dma((width // HD,)),
            dma((width // HD,)),
            dma((width // HD,)),
            dma((pairs, steps)),
            dma((pairs, steps)),
            dma((units, bits)),
            dma((units, bits)),
            dma((units,)),
            dma((units,)),
            dma((pairs, steps)),
        ],
        compiler_params=pltpu.CompilerParams(
            collective_id=0, has_side_effects=True, vmem_limit_bytes=54 * 1024 * 1024
        ),
        cost_estimate=pl.CostEstimate(
            flops=6 * tok * depth * width, bytes_accessed=12 * tok * depth, transcendentals=0
        ),
    )(inputs, qkv_weight, attn_cotangent, segment_ids.reshape(1, tok))
    return input_grad, weight_grad.T


def solution(mesh):
    return jax.shard_map(
        functools.partial(on_device, mesh.shape["inner"], mesh.shape["outer"]),
        mesh=mesh,
        in_specs=(
            P(("outer", "inner"), None),
            P(("outer", "inner"), None),
            P("inner", None),
            P(("outer", "inner"), None),
        ),
        out_specs=(P(("outer", "inner"), None), P("inner", "outer")),
        check_vma=False,
    )
```

```python
import functools
import math

import jax
import jax.numpy as jnp
from jax import lax
from jax.experimental import pallas as pl
from jax.experimental.pallas import tpu as pltpu
from jax.sharding import PartitionSpec as P

HD = 128
LAG = 2
MESH = pl.DeviceIdType.MESH


def contract(a, b, dims):
    return lax.dot_general(a, b, ((dims[:1], dims[1:]), ((), ())), preferred_element_type=jnp.float32)


def allowed_bias(seg_row, heads):
    count = seg_row.shape[1]
    seg_row = jnp.broadcast_to(seg_row.astype(jnp.float32), (count, count))
    seg_col = jnp.transpose(seg_row)
    later = lax.broadcasted_iota(jnp.int32, (count, count), 0)
    earlier = lax.broadcasted_iota(jnp.int32, (count, count), 1)
    bias = jnp.where((later >= earlier) & (seg_col == seg_row), 0.0, -1e30)
    return jnp.concatenate([bias] * heads, axis=0)


def attention_grad(query, keys, vals, cot, bias):
    scale = 1.0 / math.sqrt(HD)
    scores = contract(query, keys, (1, 1)) * scale + bias
    grad_w = contract(cot, vals, (1, 1))
    weights = jnp.exp(scores - jnp.max(scores, axis=1, keepdims=True))
    weights = weights / jnp.sum(weights, axis=1, keepdims=True)
    grad_s = weights * (grad_w - jnp.sum(weights * grad_w, axis=1, keepdims=True)) * scale
    grad_s = grad_s.astype(jnp.bfloat16)
    grad_q = contract(grad_s, keys, (1, 0))
    grad_k = contract(grad_s, query, (0, 0))
    grad_v = contract(weights.astype(jnp.bfloat16), cot, (0, 0))
    return grad_q, grad_k, grad_v


def kernel(
    n, n_outer, parts, wide, x_hbm, w_ref, cot_hbm, row_hbm, out_ref, wg_ref,
    x_ref, cot_ref, row_ref, w_all, both, acc, mine, theirs, grads, ready, back, gt, rs, got, fin, fin_got,
    copy_sem, z_send, z_recv, p_send, p_recv, s_send, s_recv, q_send, q_recv, g_send, g_recv, b_send, b_recv,
    r_send, r_recv, f_send, f_recv, o_sem,
):
    me = lax.axis_index("inner")
    o = lax.axis_index("outer")
    bits = n_outer.bit_length() - 1
    tok = x_ref.shape[0]
    bw, width = w_ref.shape
    part = bw // parts
    piece = part // n_outer
    tile = min(512, bw)
    step = min(1024, bw)
    steps = bw // step
    pairs = n // 2
    slot = me // 2
    chunks = bw // wide
    parity = me % 2
    mate = me + 1 - 2 * parity

    def bit(b):
        return (o // (1 << b)) % 2

    def across(b):
        return o + (1 - 2 * bit(b)) * (1 << b)

    started = []

    def send(cond, src, dst, s_sem, r_sem, device):
        def make():
            return pltpu.make_async_remote_copy(
                src_ref=src, dst_ref=dst, send_sem=s_sem, recv_sem=r_sem,
                device_id=device, device_id_type=MESH,
            )

        started.append((cond, make))
        if cond is None:
            make().start()
        else:
            @pl.when(cond)
            def _():
                make().start()

    def arrived(dst, r_sem):
        pltpu.make_async_remote_copy(
            src_ref=dst, dst_ref=dst, send_sem=r_sem, recv_sem=r_sem,
            device_id={"inner": (me + 1) % n}, device_id_type=MESH,
        ).wait_recv()

    own = pltpu.make_async_copy(w_ref, w_all.at[pl.ds(pl.multiple_of(slot * bw, bw), bw)], copy_sem.at[0])
    own.start()
    fetch = pltpu.make_async_copy(x_hbm, x_ref, copy_sem.at[1])
    fetch.start()
    small = [
        pltpu.make_async_copy(cot_hbm, cot_ref, copy_sem.at[2]),
        pltpu.make_async_copy(row_hbm, row_ref, copy_sem.at[3]),
    ]
    for copy in small:
        copy.start()

    barrier = pltpu.get_barrier_semaphore()
    for t in range(1, n):
        pl.semaphore_signal(barrier, inc=1, device_id={"inner": (me + t) % n}, device_id_type=MESH)
    for b in range(bits):
        pl.semaphore_signal(barrier, inc=1, device_id={"outer": across(b)}, device_id_type=MESH)
    pl.semaphore_wait(barrier, n - 1 + bits)

    def nth(t):
        return (slot + t) % pairs

    def block(i):
        return 2 * i + parity

    middle = list(range(1, bits))
    orders = [middle + [0], middle[::-1] + [0]] * 2
    groups = [[0, 1], [2, 3]] if parts == 4 else [[h] for h in range(parts)]

    def place(h):
        return sum(bit(b) * (1 << k) for k, b in enumerate(orders[h]))

    def shares(i, h, first, count):
        start = i * bw + h * part + first * piece
        return w_all.at[pl.ds(pl.multiple_of(start, piece), count * piece)]

    def z_start(t, h):
        ref = shares(slot, h, place(h), 1)
        send(None, ref, ref, z_send.at[h, nth(t)], z_recv.at[h, slot], {"inner": block(nth(t))})

    def plane_start(i, k, h):
        group = 1 << k
        ref = shares(i, h, place(h) // group * group, group)
        send(None, ref, ref, p_send.at[h, k, i], p_recv.at[h, k, i], {"outer": across(orders[h][k])})

    def plane_wait(i, k, h):
        group = 1 << k
        first = place(h) // group * group
        other = first + (1 - 2 * bit(orders[h][k])) * group
        arrived(shares(i, h, other, group), p_recv.at[h, k, i])

    def both_part(i, c):
        return both.at[pl.ds(tok, tok), pl.ds(pl.multiple_of(i * bw + c * step, step), step)]

    def swap_start(t, c):
        i = nth(t)
        src = x_ref.at[:, pl.ds(pl.multiple_of((2 * i + 1 - parity) * bw + c * step, step), step)]
        send(None, src, both_part(i, c), s_send.at[i, c], s_recv.at[i, c], {"inner": mate})

    def project(t, c):
        i = nth(t)
        arrived(both_part(i, c), s_recv.at[i, c])

        def body(r, carry):
            start = pl.multiple_of(i * bw + c * step + r * tile, tile)
            acc[...] += contract(both[:, pl.ds(start, tile)], w_all[pl.ds(start, tile), :], (1, 0))
            return carry

        lax.fori_loop(0, step // tile, body, 0)

    swaps = [(t, c) for t in range(pairs) for c in range(steps)]

    def swap_some(count):
        for t, c in swaps[:count]:
            swap_start(t, c)
        del swaps[:count]

    own.wait()
    for group in groups:
        for t in range(1, pairs):
            for h in group:
                z_start(t, h)
    fetch.wait()
    swap_some(1)
    for copy in small:
        copy.wait()
    acc[...] = jnp.zeros_like(acc)
    for i in range(pairs):
        both[:tok, i * bw : (i + 1) * bw] = x_ref[:, pl.ds(pl.multiple_of(block(i) * bw, bw), bw)]

    trips = [(t, group) for t in range(1, pairs) for group in groups]
    for turn in range(len(trips) + bits):
        for k in reversed(range(bits + 1)):
            if not 0 <= turn - k < len(trips):
                continue
            t, group = trips[turn - k]
            for h in group:
                if k == 0:
                    arrived(shares(nth(t), h, place(h), 1), z_recv.at[h, nth(t)])
                else:
                    plane_wait(nth(t), k - 1, h)
                if k < bits:
                    plane_start(nth(t), k, h)
        if turn < len(trips):
            swap_some(1 if turn < len(trips) - 1 else len(swaps))
        if turn == len(trips):
            project(0, 0)
    swap_some(len(swaps))
    for t in range(pairs):
        for c in range(steps):
            if (t, c) != (0, 0):
                project(t, c)

    heads = cot_ref.shape[1] // HD
    kv = heads * HD
    lots = [range(h, min(h + 2, heads)) for h in range(0, heads, 2)]
    spans = [(lot[0] * HD, len(lot) * HD) for lot in lots] + [(kv, 2 * HD)]
    last = len(lots)
    for p in [last] + list(range(last)):
        at = pl.ds(spans[p][0], spans[p][1])
        mine[:, at] = acc[tok:, at].astype(mine.dtype)
        send(None, mine.at[:, at], theirs.at[:, at], q_send.at[p], q_recv.at[p], {"inner": mate})

    def projected(p):
        at = pl.ds(spans[p][0], spans[p][1])
        arrived(theirs.at[:, at], q_recv.at[p])
        return (acc[:tok, at] + theirs[:, at].astype(jnp.float32)).astype(jnp.bfloat16)

    def stacked(value):
        return jnp.concatenate([value[:, h : h + HD] for h in range(0, value.shape[1], HD)], axis=0)

    def grads_out(p, value):
        start, size = spans[p]
        gt[start : start + size, :tok] = jnp.transpose(value).astype(jnp.bfloat16)
        at = pl.ds(start, size)
        send(None, gt.at[at, pl.ds(0, tok)], gt.at[at, pl.ds(tok, tok)], g_send.at[p], g_recv.at[p], {"inner": mate})
        grads[:tok, start : start + size] = value.astype(jnp.bfloat16)

    keys_vals = projected(last)
    keys, vals = keys_vals[:, :HD], keys_vals[:, HD:]
    grad_k, grad_v = 0.0, 0.0
    for p, lot in enumerate(lots):
        bias = allowed_bias(row_ref[...], len(lot))
        cot = stacked(cot_ref[:, lot[0] * HD : (lot[-1] + 1) * HD])
        grad_q, part_k, part_v = attention_grad(stacked(projected(p)), keys, vals, cot, bias)
        grad_k, grad_v = grad_k + part_k, grad_v + part_v
        grads_out(p, jnp.concatenate([grad_q[h * tok : (h + 1) * tok] for h in range(len(lot))], axis=1))
    grads_out(last, jnp.concatenate([grad_k, grad_v], axis=1))

    def write(i, c):
        src = ready.at[:, pl.ds(i * bw + c * step, step)]
        dst = out_ref.at[:, pl.ds(pl.multiple_of(block(i) * bw + c * step, step), step)]
        return pltpu.make_async_copy(src, dst, o_sem.at[i, c])

    def input_part(i, c):
        def body(r, carry):
            at = pl.ds(pl.multiple_of(i * bw + c * step + r * tile, tile), tile)
            value = contract(grads[...], w_all[at, :], (1, 1)).astype(jnp.bfloat16)
            ready[:, at] = value[:tok]
            back[:, at] = value[tok:]
            return carry

        lax.fori_loop(0, step // tile, body, 0)
        src = back.at[:, pl.ds(i * bw + c * step, step)]
        dst = out_ref.at[:, pl.ds(pl.multiple_of(block(i) * bw + c * step, step), step)]
        send(None, src, dst, b_send.at[i, c], b_recv.at[i, c], {"inner": mate})
        write(i, c).start()

    rows = width // n_outer
    units = pairs * chunks

    def pair_of(f):
        return (slot + 1 + f // chunks) % pairs

    def rs_order(f):
        return [0] + (middle if f % 2 == 0 else middle[::-1])

    def rs_region(f, k):
        base = 0
        order = rs_order(f)
        for i in range(k):
            base = base + bit(order[i]) * (width >> (i + 1))
        half = width >> (k + 1)
        b = bit(order[k])
        return base + b * half, base + (1 - b) * half, half

    def got_at(f, k, half):
        return got.at[f, pl.ds(width - (width >> k), half)]

    def rs_start(f, k):
        keep, give, half = rs_region(f, k)
        src = rs.at[f, pl.ds(pl.multiple_of(give, rows), half)]
        send(None, src, got_at(f, k, half), r_send.at[f, k], r_recv.at[f, k], {"outer": across(rs_order(f)[k])})

    def rs_add(f, k):
        keep, give, half = rs_region(f, k)
        arrived(got_at(f, k, half), r_recv.at[f, k])
        at = pl.ds(pl.multiple_of(keep, rows), half)
        total = rs[f, at, :].astype(jnp.float32) + got[f, pl.ds(width - (width >> k), half), :].astype(jnp.float32)
        if k < bits - 1:
            rs[f, at, :] = total.astype(rs.dtype)
            return
        turn, c = f // chunks, f % chunks
        if turn < pairs - 1:
            fin[f] = total.astype(fin.dtype)
            owner = 2 * pair_of(f) + parity
            send(None, fin.at[f], fin_got.at[f], f_send.at[f], f_recv.at[f], {"inner": owner})
        else:
            for other in range(pairs - 1):
                spot = other * chunks + c
                arrived(fin_got.at[spot], f_recv.at[spot])
                total += fin_got[spot].astype(jnp.float32)
            wg_ref[:, c * wide : (c + 1) * wide] = total

    def weight_part(f):
        if f == 0:
            for p, (start, size) in enumerate(spans):
                arrived(gt.at[pl.ds(start, size), pl.ds(tok, tok)], g_recv.at[p])
        order = rs_order(f)
        start = pl.multiple_of(pair_of(f) * bw + (f % chunks) * wide, 128)
        product = contract(gt[...], both[:, pl.ds(start, wide)], (1, 0))
        for g in range(n_outer):
            spot = sum(((g >> b) & 1) << (bits - 1 - k) for k, b in enumerate(order))
            rs[f, spot * rows : (spot + 1) * rows, :] = product[g * rows : (g + 1) * rows].astype(rs.dtype)

    inputs = [(i, c) for i in range(pairs) for c in range(steps)]
    backs = list(inputs)
    lags = [0] + [1 + LAG * k for k in range(bits)]
    for turn in range(units // 2 + lags[-1]):
        for k in reversed(range(bits + 1)):
            for f in (2 * (turn - lags[k]), 2 * (turn - lags[k]) + 1):
                if not 0 <= f < units:
                    continue
                if k == 0:
                    weight_part(f)
                else:
                    rs_add(f, k - 1)
                if k < bits:
                    rs_start(f, k)
        if turn == 0:
            grads[tok:, :] = jnp.transpose(gt[:, tok:].astype(jnp.float32)).astype(jnp.bfloat16)
        if backs:
            input_part(*backs.pop(0))
    for i, c in backs:
        input_part(i, c)
    for i, c in inputs:
        spot = (2 * i + 1 - parity) * bw + c * step
        arrived(out_ref.at[:, pl.ds(pl.multiple_of(spot, step), step)], b_recv.at[i, c])
        write(i, c).wait()

    for cond, make in started:
        if cond is None:
            make().wait_send()
        else:
            @pl.when(cond)
            def _():
                make().wait_send()


def on_device(n, n_outer, inputs, segment_ids, qkv_weight, attn_cotangent):
    tok, depth = inputs.shape
    bw, width = qkv_weight.shape
    bits = n_outer.bit_length() - 1
    parts = 4 if bw % (64 * n_outer) == 0 else 1
    steps = bw // min(1024, bw)
    rows = width // n_outer
    wire = jnp.bfloat16 if rows % 16 == 0 else jnp.float32
    wide = min(256, bw // 2)
    pairs = n // 2
    units = pairs * bw // wide
    vmem = pl.BlockSpec(memory_space=pltpu.VMEM)
    hbm = pl.BlockSpec(memory_space=pltpu.HBM)
    dma = pltpu.SemaphoreType.DMA
    input_grad, weight_grad = pl.pallas_call(
        functools.partial(kernel, n, n_outer, parts, wide),
        out_shape=(
            jax.ShapeDtypeStruct((tok, depth), jnp.bfloat16),
            jax.ShapeDtypeStruct((rows, bw), jnp.float32),
        ),
        in_specs=[hbm] * 4,
        out_specs=(hbm, vmem),
        scratch_shapes=[
            pltpu.VMEM((tok, depth), jnp.bfloat16),
            pltpu.VMEM(attn_cotangent.shape, jnp.bfloat16),
            pltpu.VMEM((1, tok), jnp.int32),
            pltpu.VMEM((pairs * bw, width), jnp.bfloat16),
            pltpu.VMEM((2 * tok, pairs * bw), jnp.bfloat16),
            pltpu.VMEM((2 * tok, width), jnp.float32),
            pltpu.VMEM((tok, width), jnp.bfloat16),
            pltpu.VMEM((tok, width), jnp.bfloat16),
            pltpu.VMEM((2 * tok, width), jnp.bfloat16),
            pltpu.VMEM((tok, pairs * bw), jnp.bfloat16),
            pltpu.VMEM((tok, pairs * bw), jnp.bfloat16),
            pltpu.VMEM((width, 2 * tok), jnp.bfloat16),
            pltpu.VMEM((units, width, wide), wire),
            pltpu.VMEM((units, width, wide), wire),
            pltpu.VMEM((units, rows, wide), wire),
            pltpu.VMEM((units, rows, wide), wire),
            dma((4,)),
            dma((parts, pairs)),
            dma((parts, pairs)),
            dma((parts, bits, pairs)),
            dma((parts, bits, pairs)),
            dma((pairs, steps)),
            dma((pairs, steps)),
            dma((width // HD,)),
            dma((width // HD,)),
            dma((width // HD,)),
            dma((width // HD,)),
            dma((pairs, steps)),
            dma((pairs, steps)),
            dma((units, bits)),
            dma((units, bits)),
            dma((units,)),
            dma((units,)),
            dma((pairs, steps)),
        ],
        compiler_params=pltpu.CompilerParams(
            collective_id=0, has_side_effects=True, vmem_limit_bytes=54 * 1024 * 1024
        ),
        cost_estimate=pl.CostEstimate(
            flops=6 * tok * depth * width, bytes_accessed=12 * tok * depth, transcendentals=0
        ),
    )(inputs, qkv_weight, attn_cotangent, segment_ids.reshape(1, tok))
    return input_grad, weight_grad.T


def solution(mesh):
    return jax.shard_map(
        functools.partial(on_device, mesh.shape["inner"], mesh.shape["outer"]),
        mesh=mesh,
        in_specs=(
            P(("outer", "inner"), None),
            P(("outer", "inner"), None),
            P("inner", None),
            P(("outer", "inner"), None),
        ),
        out_specs=(P(("outer", "inner"), None), P("inner", "outer")),
        check_vma=False,
    )
```

```python
import functools
import math

import jax
import jax.numpy as jnp
from jax import lax
from jax.experimental import pallas as pl
from jax.experimental.pallas import tpu as pltpu
from jax.sharding import PartitionSpec as P

HD = 128
LAG = 2
MESH = pl.DeviceIdType.MESH


def contract(a, b, dims):
    return lax.dot_general(a, b, ((dims[:1], dims[1:]), ((), ())), preferred_element_type=jnp.float32)


def allowed_bias(seg_row, heads):
    count = seg_row.shape[1]
    seg_row = jnp.broadcast_to(seg_row.astype(jnp.float32), (count, count))
    seg_col = jnp.transpose(seg_row)
    later = lax.broadcasted_iota(jnp.int32, (count, count), 0)
    earlier = lax.broadcasted_iota(jnp.int32, (count, count), 1)
    bias = jnp.where((later >= earlier) & (seg_col == seg_row), 0.0, -1e30)
    return jnp.concatenate([bias] * heads, axis=0)


def attention_grad(query, keys, vals, cot, bias):
    scale = 1.0 / math.sqrt(HD)
    scores = contract(query, keys, (1, 1)) * scale + bias
    grad_w = contract(cot, vals, (1, 1))
    weights = jnp.exp(scores - jnp.max(scores, axis=1, keepdims=True))
    weights = weights / jnp.sum(weights, axis=1, keepdims=True)
    grad_s = weights * (grad_w - jnp.sum(weights * grad_w, axis=1, keepdims=True)) * scale
    grad_s = grad_s.astype(jnp.bfloat16)
    grad_q = contract(grad_s, keys, (1, 0))
    grad_k = contract(grad_s, query, (0, 0))
    grad_v = contract(weights.astype(jnp.bfloat16), cot, (0, 0))
    return grad_q, grad_k, grad_v


def kernel(
    n, n_outer, parts, wide, x_hbm, w_ref, cot_hbm, row_hbm, out_ref, wg_ref,
    x_ref, cot_ref, row_ref, w_all, both, acc, mine, theirs, grads, ready, back, gt, rs, got, fin, fin_got,
    copy_sem, z_send, z_recv, p_send, p_recv, s_send, s_recv, q_send, q_recv, g_send, g_recv, b_send, b_recv,
    r_send, r_recv, f_send, f_recv, o_sem,
):
    me = lax.axis_index("inner")
    o = lax.axis_index("outer")
    bits = n_outer.bit_length() - 1
    tok = x_ref.shape[0]
    bw, width = w_ref.shape
    part = bw // parts
    piece = part // n_outer
    tile = min(512, bw)
    step = min(1024, bw)
    steps = bw // step
    pairs = n // 2
    slot = me // 2
    chunks = bw // wide
    parity = me % 2
    mate = me + 1 - 2 * parity

    def bit(b):
        return (o // (1 << b)) % 2

    def across(b):
        return o + (1 - 2 * bit(b)) * (1 << b)

    started = []

    def send(cond, src, dst, s_sem, r_sem, device):
        def make():
            return pltpu.make_async_remote_copy(
                src_ref=src, dst_ref=dst, send_sem=s_sem, recv_sem=r_sem,
                device_id=device, device_id_type=MESH,
            )

        started.append((cond, make))
        if cond is None:
            make().start()
        else:
            @pl.when(cond)
            def _():
                make().start()

    def arrived(dst, r_sem):
        pltpu.make_async_remote_copy(
            src_ref=dst, dst_ref=dst, send_sem=r_sem, recv_sem=r_sem,
            device_id={"inner": (me + 1) % n}, device_id_type=MESH,
        ).wait_recv()

    own = pltpu.make_async_copy(w_ref, w_all.at[pl.ds(pl.multiple_of(slot * bw, bw), bw)], copy_sem.at[0])
    own.start()
    fetch = pltpu.make_async_copy(x_hbm, x_ref, copy_sem.at[1])
    fetch.start()
    small = [
        pltpu.make_async_copy(cot_hbm, cot_ref, copy_sem.at[2]),
        pltpu.make_async_copy(row_hbm, row_ref, copy_sem.at[3]),
    ]
    for copy in small:
        copy.start()

    barrier = pltpu.get_barrier_semaphore()
    for t in range(1, n):
        pl.semaphore_signal(barrier, inc=1, device_id={"inner": (me + t) % n}, device_id_type=MESH)
    for b in range(bits):
        pl.semaphore_signal(barrier, inc=1, device_id={"outer": across(b)}, device_id_type=MESH)
    pl.semaphore_wait(barrier, n - 1 + bits)

    def nth(t):
        return (slot + t) % pairs

    def block(i):
        return 2 * i + parity

    middle = list(range(1, bits))
    orders = [middle + [0], middle[::-1] + [0]] * 2
    groups = [[0, 1], [2, 3]] if parts == 4 else [[h] for h in range(parts)]

    def place(h):
        return sum(bit(b) * (1 << k) for k, b in enumerate(orders[h]))

    def shares(i, h, first, count):
        start = i * bw + h * part + first * piece
        return w_all.at[pl.ds(pl.multiple_of(start, piece), count * piece)]

    def z_start(t, h):
        ref = shares(slot, h, place(h), 1)
        send(None, ref, ref, z_send.at[h, nth(t)], z_recv.at[h, slot], {"inner": block(nth(t))})

    def plane_start(i, k, h):
        group = 1 << k
        ref = shares(i, h, place(h) // group * group, group)
        send(None, ref, ref, p_send.at[h, k, i], p_recv.at[h, k, i], {"outer": across(orders[h][k])})

    def plane_wait(i, k, h):
        group = 1 << k
        first = place(h) // group * group
        other = first + (1 - 2 * bit(orders[h][k])) * group
        arrived(shares(i, h, other, group), p_recv.at[h, k, i])

    def both_part(i, c):
        return both.at[pl.ds(tok, tok), pl.ds(pl.multiple_of(i * bw + c * step, step), step)]

    def swap_start(t, c):
        i = nth(t)
        src = x_ref.at[:, pl.ds(pl.multiple_of((2 * i + 1 - parity) * bw + c * step, step), step)]
        send(None, src, both_part(i, c), s_send.at[i, c], s_recv.at[i, c], {"inner": mate})

    def project(t, c):
        i = nth(t)
        arrived(both_part(i, c), s_recv.at[i, c])

        def body(r, carry):
            start = pl.multiple_of(i * bw + c * step + r * tile, tile)
            acc[...] += contract(both[:, pl.ds(start, tile)], w_all[pl.ds(start, tile), :], (1, 0))
            return carry

        lax.fori_loop(0, step // tile, body, 0)

    swaps = [(t, c) for t in range(pairs) for c in range(steps)]

    def swap_some(count):
        for t, c in swaps[:count]:
            swap_start(t, c)
        del swaps[:count]

    own.wait()
    for group in groups:
        for t in range(1, pairs):
            for h in group:
                z_start(t, h)
    fetch.wait()
    swap_some(1)
    for copy in small:
        copy.wait()
    acc[...] = jnp.zeros_like(acc)
    for i in range(pairs):
        both[:tok, i * bw : (i + 1) * bw] = x_ref[:, pl.ds(pl.multiple_of(block(i) * bw, bw), bw)]

    trips = [(t, group) for t in range(1, pairs) for group in groups]
    for turn in range(len(trips) + bits):
        for k in reversed(range(bits + 1)):
            if not 0 <= turn - k < len(trips):
                continue
            t, group = trips[turn - k]
            for h in group:
                if k == 0:
                    arrived(shares(nth(t), h, place(h), 1), z_recv.at[h, nth(t)])
                else:
                    plane_wait(nth(t), k - 1, h)
                if k < bits:
                    plane_start(nth(t), k, h)
        if turn < len(trips):
            swap_some(1 if turn < len(trips) - 1 else len(swaps))
        if turn == len(trips):
            project(0, 0)
    swap_some(len(swaps))
    for t in range(pairs):
        for c in range(steps):
            if (t, c) != (0, 0):
                project(t, c)

    heads = cot_ref.shape[1] // HD
    kv = heads * HD
    lots = [range(h, min(h + 2, heads)) for h in range(0, heads, 2)]
    spans = [(lot[0] * HD, len(lot) * HD) for lot in lots] + [(kv, 2 * HD)]
    last = len(lots)
    for p in [last] + list(range(last)):
        at = pl.ds(spans[p][0], spans[p][1])
        mine[:, at] = acc[tok:, at].astype(mine.dtype)
        send(None, mine.at[:, at], theirs.at[:, at], q_send.at[p], q_recv.at[p], {"inner": mate})

    def projected(p):
        at = pl.ds(spans[p][0], spans[p][1])
        arrived(theirs.at[:, at], q_recv.at[p])
        return (acc[:tok, at] + theirs[:, at].astype(jnp.float32)).astype(jnp.bfloat16)

    def stacked(value):
        return jnp.concatenate([value[:, h : h + HD] for h in range(0, value.shape[1], HD)], axis=0)

    def grads_out(p, value):
        start, size = spans[p]
        gt[start : start + size, :tok] = jnp.transpose(value).astype(jnp.bfloat16)
        at = pl.ds(start, size)
        send(None, gt.at[at, pl.ds(0, tok)], gt.at[at, pl.ds(tok, tok)], g_send.at[p], g_recv.at[p], {"inner": mate})
        grads[:tok, start : start + size] = value.astype(jnp.bfloat16)

    keys_vals = projected(last)
    keys, vals = keys_vals[:, :HD], keys_vals[:, HD:]
    grad_k, grad_v = 0.0, 0.0
    for p, lot in enumerate(lots):
        bias = allowed_bias(row_ref[...], len(lot))
        cot = stacked(cot_ref[:, lot[0] * HD : (lot[-1] + 1) * HD])
        grad_q, part_k, part_v = attention_grad(stacked(projected(p)), keys, vals, cot, bias)
        grad_k, grad_v = grad_k + part_k, grad_v + part_v
        grads_out(p, jnp.concatenate([grad_q[h * tok : (h + 1) * tok] for h in range(len(lot))], axis=1))
    grads_out(last, jnp.concatenate([grad_k, grad_v], axis=1))

    def write(i, c):
        src = ready.at[:, pl.ds(i * bw + c * step, step)]
        dst = out_ref.at[:, pl.ds(pl.multiple_of(block(i) * bw + c * step, step), step)]
        return pltpu.make_async_copy(src, dst, o_sem.at[i, c])

    def input_part(i, c):
        def body(r, carry):
            at = pl.ds(pl.multiple_of(i * bw + c * step + r * tile, tile), tile)
            value = contract(grads[...], w_all[at, :], (1, 1)).astype(jnp.bfloat16)
            ready[:, at] = value[:tok]
            back[:, at] = value[tok:]
            return carry

        lax.fori_loop(0, step // tile, body, 0)
        src = back.at[:, pl.ds(i * bw + c * step, step)]
        dst = out_ref.at[:, pl.ds(pl.multiple_of(block(i) * bw + c * step, step), step)]
        send(None, src, dst, b_send.at[i, c], b_recv.at[i, c], {"inner": mate})
        write(i, c).start()

    rows = width // n_outer
    units = pairs * chunks

    def pair_of(f):
        return (slot + 1 + f // chunks) % pairs

    def rs_order(f):
        return [0] + (middle if f % 2 == 0 else middle[::-1])

    def rs_region(f, k):
        base = 0
        order = rs_order(f)
        for i in range(k):
            base = base + bit(order[i]) * (width >> (i + 1))
        half = width >> (k + 1)
        b = bit(order[k])
        return base + b * half, base + (1 - b) * half, half

    def got_at(f, k, half):
        return got.at[f, pl.ds(width - (width >> k), half)]

    def rs_start(f, k):
        keep, give, half = rs_region(f, k)
        src = rs.at[f, pl.ds(pl.multiple_of(give, rows), half)]
        send(None, src, got_at(f, k, half), r_send.at[f, k], r_recv.at[f, k], {"outer": across(rs_order(f)[k])})

    def rs_add(f, k):
        keep, give, half = rs_region(f, k)
        arrived(got_at(f, k, half), r_recv.at[f, k])
        at = pl.ds(pl.multiple_of(keep, rows), half)
        total = rs[f, at, :].astype(jnp.float32) + got[f, pl.ds(width - (width >> k), half), :].astype(jnp.float32)
        if k < bits - 1:
            rs[f, at, :] = total.astype(rs.dtype)
            return
        turn, c = f // chunks, f % chunks
        if turn < pairs - 1:
            fin[f] = total.astype(fin.dtype)
            owner = 2 * pair_of(f) + parity
            send(None, fin.at[f], fin_got.at[f], f_send.at[f], f_recv.at[f], {"inner": owner})
        else:
            for other in range(pairs - 1):
                spot = other * chunks + c
                arrived(fin_got.at[spot], f_recv.at[spot])
                total += fin_got[spot].astype(jnp.float32)
            wg_ref[:, c * wide : (c + 1) * wide] = total

    def weight_part(f):
        order = rs_order(f)
        start = pl.multiple_of(pair_of(f) * bw + (f % chunks) * wide, 128)
        product = contract(gt[...], both[:, pl.ds(start, wide)], (1, 0))
        for g in range(n_outer):
            spot = sum(((g >> b) & 1) << (bits - 1 - k) for k, b in enumerate(order))
            rs[f, spot * rows : (spot + 1) * rows, :] = product[g * rows : (g + 1) * rows].astype(rs.dtype)

    inputs = [(i, c) for i in range(pairs) for c in range(steps)]
    backs = list(inputs)
    for p, (start, size) in enumerate(spans):
        arrived(gt.at[pl.ds(start, size), pl.ds(tok, tok)], g_recv.at[p])
        grads[tok:, start : start + size] = jnp.transpose(
            gt[start : start + size, tok:].astype(jnp.float32)
        ).astype(jnp.bfloat16)
    input_part(*backs.pop(0))
    lags = [0] + [1 + LAG * k for k in range(bits)]
    for turn in range(units // 2 + lags[-1]):
        for k in reversed(range(bits + 1)):
            for f in (2 * (turn - lags[k]), 2 * (turn - lags[k]) + 1):
                if not 0 <= f < units:
                    continue
                if k == 0:
                    weight_part(f)
                else:
                    rs_add(f, k - 1)
                if k < bits:
                    rs_start(f, k)
        if backs and turn:
            input_part(*backs.pop(0))
    for i, c in backs:
        input_part(i, c)
    for i, c in inputs:
        spot = (2 * i + 1 - parity) * bw + c * step
        arrived(out_ref.at[:, pl.ds(pl.multiple_of(spot, step), step)], b_recv.at[i, c])
        write(i, c).wait()

    for cond, make in started:
        if cond is None:
            make().wait_send()
        else:
            @pl.when(cond)
            def _():
                make().wait_send()


def on_device(n, n_outer, inputs, segment_ids, qkv_weight, attn_cotangent):
    tok, depth = inputs.shape
    bw, width = qkv_weight.shape
    bits = n_outer.bit_length() - 1
    parts = 4 if bw % (64 * n_outer) == 0 else 1
    steps = bw // min(1024, bw)
    rows = width // n_outer
    wire = jnp.bfloat16 if rows % 16 == 0 else jnp.float32
    wide = min(256, bw // 2)
    pairs = n // 2
    units = pairs * bw // wide
    vmem = pl.BlockSpec(memory_space=pltpu.VMEM)
    hbm = pl.BlockSpec(memory_space=pltpu.HBM)
    dma = pltpu.SemaphoreType.DMA
    input_grad, weight_grad = pl.pallas_call(
        functools.partial(kernel, n, n_outer, parts, wide),
        out_shape=(
            jax.ShapeDtypeStruct((tok, depth), jnp.bfloat16),
            jax.ShapeDtypeStruct((rows, bw), jnp.float32),
        ),
        in_specs=[hbm] * 4,
        out_specs=(hbm, vmem),
        scratch_shapes=[
            pltpu.VMEM((tok, depth), jnp.bfloat16),
            pltpu.VMEM(attn_cotangent.shape, jnp.bfloat16),
            pltpu.VMEM((1, tok), jnp.int32),
            pltpu.VMEM((pairs * bw, width), jnp.bfloat16),
            pltpu.VMEM((2 * tok, pairs * bw), jnp.bfloat16),
            pltpu.VMEM((2 * tok, width), jnp.float32),
            pltpu.VMEM((tok, width), jnp.bfloat16),
            pltpu.VMEM((tok, width), jnp.bfloat16),
            pltpu.VMEM((2 * tok, width), jnp.bfloat16),
            pltpu.VMEM((tok, pairs * bw), jnp.bfloat16),
            pltpu.VMEM((tok, pairs * bw), jnp.bfloat16),
            pltpu.VMEM((width, 2 * tok), jnp.bfloat16),
            pltpu.VMEM((units, width, wide), wire),
            pltpu.VMEM((units, width, wide), wire),
            pltpu.VMEM((units, rows, wide), wire),
            pltpu.VMEM((units, rows, wide), wire),
            dma((4,)),
            dma((parts, pairs)),
            dma((parts, pairs)),
            dma((parts, bits, pairs)),
            dma((parts, bits, pairs)),
            dma((pairs, steps)),
            dma((pairs, steps)),
            dma((width // HD,)),
            dma((width // HD,)),
            dma((width // HD,)),
            dma((width // HD,)),
            dma((pairs, steps)),
            dma((pairs, steps)),
            dma((units, bits)),
            dma((units, bits)),
            dma((units,)),
            dma((units,)),
            dma((pairs, steps)),
        ],
        compiler_params=pltpu.CompilerParams(
            collective_id=0, has_side_effects=True, vmem_limit_bytes=54 * 1024 * 1024
        ),
        cost_estimate=pl.CostEstimate(
            flops=6 * tok * depth * width, bytes_accessed=12 * tok * depth, transcendentals=0
        ),
    )(inputs, qkv_weight, attn_cotangent, segment_ids.reshape(1, tok))
    return input_grad, weight_grad.T


def solution(mesh):
    return jax.shard_map(
        functools.partial(on_device, mesh.shape["inner"], mesh.shape["outer"]),
        mesh=mesh,
        in_specs=(
            P(("outer", "inner"), None),
            P(("outer", "inner"), None),
            P("inner", None),
            P(("outer", "inner"), None),
        ),
        out_specs=(P(("outer", "inner"), None), P("inner", "outer")),
        check_vma=False,
    )
```
